256 devices in a mesh: gx: 32 (over y_hi, z, core), gy: 8 (over x, y_lo).
Axes of the slice: x: 4, y: 4 (y_hi: 2, y_lo: 2; y = y_hi * 2 + y_lo), z: 8, core: 2. Of those that a mesh axis runs over, the one named last changes fastest.
Arguments:
- flow_speed_vectors: float32 [3, 10, 2048, 2048], P(None, None, 'gx', 'gy'), may hold values from -6 to 6
- thermal_state: float32 [10, 2048, 2048], P(None, 'gx', 'gy'), may hold values from 0.5 to 2
- northward_basis_matrix: bfloat16 [2048, 256], P('gy'), may hold values from -0.125 to 0.125
Outputs:
- gram: float32 [2048, 2048], P('gx')
The draws below stay inside these ranges and needn't reach their ends.
All inputs are finite; a program needn't handle non-finite values.
Results may differ from the reference program's by a relative error of at most 0.0003.
Values may be sent and summed in bfloat16 or wider, within the bound.
No kernel may reach another device: no remote copies, remote signals or barrier semaphores. Data moves between devices by JAX's collectives and lax.ppermute only.
A program may use at most 64 MiB of HBM per device.

```python
import jax
import jax.numpy as jnp
from jax import lax

GRID_WIDTH_EAST = 2048
GRID_WIDTH_NORTH = 2048
R = 256
Z = 6
DEPTH_WITH_HALO = 10


def steps_of(own_key, shape, split, smallest, top_value):
    loudness = 1.0
    for axis_at, blocks in split:
        heights = jax.random.uniform(jax.random.fold_in(jax.random.fold_in(own_key, 6), axis_at), (blocks,), jnp.float32, smallest / len(split), top_value / len(split))
        loudness = loudness * jnp.repeat(jnp.exp(heights), shape[axis_at] // blocks).reshape((-1,) + (1,) * (len(shape) - 1 - axis_at))
    return loudness


def noise(rng, shape, width, bound, pieces=(), kind=jnp.bfloat16):
    array = width * jax.random.normal(rng, shape, jnp.float32)
    if pieces:
        array = array * steps_of(rng, shape, pieces, -0.22, 0.18)
    return jnp.clip(array, -bound, bound).astype(kind)


def setup_inputs(seed: int = 0) -> dict:
    arg_keys = jax.random.split(jax.random.key(seed), 4)
    return {
        "flow_speed_vectors": noise(arg_keys[0], (3, DEPTH_WITH_HALO, GRID_WIDTH_EAST, GRID_WIDTH_NORTH), 1.0, 6.0, ((2, 32), (3, 8)), jnp.float32),
        "thermal_state": jnp.clip(0.5 + 1.5 * jax.random.uniform(arg_keys[1], (DEPTH_WITH_HALO, GRID_WIDTH_EAST, GRID_WIDTH_NORTH), jnp.float32) ** steps_of(arg_keys[1], (DEPTH_WITH_HALO, GRID_WIDTH_EAST, GRID_WIDTH_NORTH), ((1, 32), (2, 8)), -0.2, 0.2), 0.5, 2.0),
        "northward_basis_matrix": noise(arg_keys[2], (GRID_WIDTH_NORTH, R), GRID_WIDTH_NORTH ** -0.5, 0.125, ((0, 8),)),
    }


def energy_loss_rate(partial_derivatives, thermal_state):
    deformation_norm = jnp.zeros_like(thermal_state)
    for source in range(3):
        for target in range(3):
            strain = 0.5 * (partial_derivatives[source][target] + partial_derivatives[target][source])
            deformation_norm = deformation_norm + strain * strain
    flow_expansion = partial_derivatives[0][0] + partial_derivatives[1][1] + partial_derivatives[2][2]
    return 0.1 * thermal_state ** 0.7 * (2.0 * deformation_norm - (2.0 / 3.0) * flow_expansion * flow_expansion)


def periodic_deriv(pointwise_quantity, axis):
    ahead_two = jnp.roll(pointwise_quantity, -2, axis)
    ahead_one = jnp.roll(pointwise_quantity, -1, axis)
    behind_one = jnp.roll(pointwise_quantity, 1, axis)
    behind_two = jnp.roll(pointwise_quantity, 2, axis)
    return (-ahead_two + 8.0 * ahead_one - 8.0 * behind_one + behind_two) / 12.0


def reference(flow_speed_vectors, thermal_state, northward_basis_matrix):
    def plane(depth_position):
        slab = lax.dynamic_slice_in_dim(flow_speed_vectors, depth_position, 5, 1)
        center = slab[:, 2]
        deriv_z = (-slab[:, 4] + 8.0 * slab[:, 3] - 8.0 * slab[:, 1] + slab[:, 0]) / 12.0
        deriv_x = periodic_deriv(center, 1)
        deriv_y = periodic_deriv(center, 2)
        partial_derivatives = [[deriv_z[comp], deriv_x[comp], deriv_y[comp]] for comp in range(3)]
        thermal_output = lax.dynamic_slice_in_dim(thermal_state, depth_position + 2, 1, 0)[0]
        pointwise_quantity = energy_loss_rate(partial_derivatives, thermal_output).astype(jnp.bfloat16)
        return jnp.dot(pointwise_quantity, northward_basis_matrix, preferred_element_type=jnp.float32)

    planes = lax.map(plane, jnp.arange(Z, dtype=jnp.int32))
    core = jnp.transpose(planes, (1, 0, 2)).astype(jnp.bfloat16).reshape(GRID_WIDTH_EAST, Z * R)
    gram = lax.dot_general(core, core, (((1,), (1,)), ((), ())), preferred_element_type=jnp.float32)
    return gram * (1.0 / (Z * R))
```

```python
import jax
import jax.numpy as jnp
from jax import lax
from jax.experimental import pallas as pl
from jax.experimental.pallas import tpu as pltpu
from jax.sharding import Mesh
from jax.sharding import PartitionSpec as P

VMEM = pl.BlockSpec(memory_space=pltpu.VMEM)
NEAR = ("core", "x", "y_lo")
FAR = ("y_hi", "z")
EAST = ("y_hi", "z", "core")
NORTH = ("x", "y_lo")
LIMIT = 48 * 1024 * 1024


def params():
    return pltpu.CompilerParams(vmem_limit_bytes=LIMIT)


def shifted(value, axes, step):
    count = lax.axis_size(axes)
    return lax.ppermute(value, axes, [(k, (k + step) % count) for k in range(count)])


def faces_kernel(flow, x_first, x_last, y_first, y_last):
    planes = x_first.shape[1]
    lane = lax.broadcasted_iota(jnp.int32, y_first.shape, 1)
    first = jnp.zeros(y_first.shape, jnp.float32)
    last = jnp.zeros(y_first.shape, jnp.float32)
    width = flow.shape[3]
    rows = flow.shape[2]
    for comp in range(3):
        for plane in range(planes):
            x_first[comp, plane] = flow[comp, plane + 2, 0:2, :]
            x_last[comp, plane] = flow[comp, plane + 2, rows - 2 : rows, :]
            at = 2 * (comp * planes + plane)
            here = (lane == at) | (lane == at + 1)
            low = flow[comp, plane + 2, :, 0:128]
            high = flow[comp, plane + 2, :, width - 128 : width]
            first = jnp.where(here, pltpu.roll(low, at, 1) if at else low, first)
            last = jnp.where(here, pltpu.roll(high, (at + 2) % 128, 1), last)
    y_first[...] = first
    y_last[...] = last


def difference(ahead_two, ahead_one, behind_one, behind_two):
    return (8.0 * (ahead_one - behind_one) - (ahead_two - behind_two)) * (1.0 / 12.0)


def field_kernel(flow, thermal, basis, x_low, x_high, y_low, y_high, out, padded):
    planes = thermal.shape[0] - 4
    rows, width = thermal.shape[1], thermal.shape[2]
    rank = basis.shape[1]
    matrix = basis[...]
    lane = lax.broadcasted_iota(jnp.int32, (rows, 128), 1)
    for plane in range(planes):
        grads = []
        for comp in range(3):
            here = flow[comp, plane + 2]
            along_z = difference(
                flow[comp, plane + 4], flow[comp, plane + 3], flow[comp, plane + 1], flow[comp, plane]
            )
            padded[comp, 8 : 8 + rows, :] = here
            padded[comp, 6:8, :] = x_low[comp, plane]
            padded[comp, 8 + rows : 10 + rows, :] = x_high[comp, plane]
            along_x = difference(
                padded[comp, 10 : 10 + rows, :],
                padded[comp, 9 : 9 + rows, :],
                padded[comp, 7 : 7 + rows, :],
                padded[comp, 6 : 6 + rows, :],
            )
            at = 2 * (comp * planes + plane)
            low = pltpu.roll(y_low[...], 126 - at, 1)
            high = pltpu.roll(y_high[...], (128 - at) % 128, 1) if at else y_high[...]
            halo = jnp.where(lane < 64, high, low)
            wide = jnp.concatenate([here, halo], axis=1)
            total = width + 128
            along_y = difference(
                pltpu.roll(wide, total - 2, 1)[:, :width],
                pltpu.roll(wide, total - 1, 1)[:, :width],
                pltpu.roll(wide, 1, 1)[:, :width],
                pltpu.roll(wide, 2, 1)[:, :width],
            )
            grads.append((along_z, along_x, along_y))
        diagonal = grads[0][0] * grads[0][0] + grads[1][1] * grads[1][1] + grads[2][2] * grads[2][2]
        cross = None
        for a, b in ((0, 1), (0, 2), (1, 2)):
            both = grads[a][b] + grads[b][a]
            cross = both * both if cross is None else cross + both * both
        expansion = grads[0][0] + grads[1][1] + grads[2][2]
        rate = 2.0 * diagonal + cross - (2.0 / 3.0) * (expansion * expansion)
        field = 0.1 * jnp.exp(0.7 * jnp.log(thermal[plane + 2])) * rate
        out[:, plane * rank : (plane + 1) * rank] = jnp.dot(
            field.astype(jnp.bfloat16), matrix, preferred_element_type=jnp.float32
        )


def sum_kernel(parts, near, far):
    total = parts[0]
    for part in range(1, parts.shape[0]):
        total = total + parts[part]
    piece = total.astype(jnp.bfloat16)
    for at in range(near.shape[0]):
        near[at] = piece
    for at in range(far.shape[0]):
        far[at] = piece


def block_kernel(scale, left, right, out):
    count, piece, depth = left.shape
    a = left[...].reshape(count * piece, depth)
    w = right[...].reshape(right.shape[0] * piece, depth)
    block = lax.dot_general(w, a, (((1,), (1,)), ((), ())), preferred_element_type=jnp.float32)
    block = block * scale
    half = block.shape[0] // 2
    side = block.shape[1] // 2
    top, bottom = block[:half], block[half:]
    first = jnp.concatenate([top[:, :side], bottom[:, :side]], axis=1)
    second = jnp.concatenate([top[:, side:], bottom[:, side:]], axis=1)
    copies = out.shape[0] // 2
    for at in range(copies):
        out[at] = first
        out[copies + at] = second


def place_kernel(piece, blocks, out):
    count, half, _ = blocks.shape
    tiles = half // piece
    side = out.shape[0]
    for tile in range(tiles):
        stacked = jnp.concatenate(
            [blocks[at, tile * piece : (tile + 1) * piece, :] for at in range(count)], axis=0
        )
        turned = stacked.T
        out[:, tile * 128 : (tile + 1) * 128] = turned[:side]
        out[:, (tiles + tile) * 128 : (tiles + tile + 1) * 128] = turned[side:]


def body(flow, thermal, basis):
    planes = thermal.shape[0] - 4
    rows, width = thermal.shape[1], thermal.shape[2]
    rank = basis.shape[1]
    f32 = jnp.float32
    x_face = jax.ShapeDtypeStruct((3, planes, 2, width), f32)
    y_face = jax.ShapeDtypeStruct((rows, 128), f32)
    x_first, x_last, y_first, y_last = pl.pallas_call(
        faces_kernel,
        out_shape=(x_face, x_face, y_face, y_face),
        in_specs=[VMEM],
        out_specs=(VMEM,) * 4,
        compiler_params=params(),
        name="faces",
    )(flow)
    x_low = shifted(x_last, EAST, 1)
    x_high = shifted(x_first, EAST, -1)
    y_low = shifted(y_last, NORTH, 1)
    y_high = shifted(y_first, NORTH, -1)
    partial = pl.pallas_call(
        field_kernel,
        out_shape=jax.ShapeDtypeStruct((rows, planes * rank), f32),
        in_specs=[VMEM] * 7,
        out_specs=VMEM,
        scratch_shapes=[pltpu.VMEM((3, rows + 16, width), f32)],
        compiler_params=params(),
        name="field",
    )(flow, thermal, basis, x_low, x_high, y_low, y_high)
    north = lax.axis_size(NORTH)
    near = lax.axis_size(NEAR)
    far = lax.axis_size(FAR)
    piece = rows // north
    depth = planes * rank
    parts = lax.all_to_all(partial.reshape(north, piece, depth), NORTH, 0, 0)
    to_near, to_far = pl.pallas_call(
        sum_kernel,
        out_shape=(
            jax.ShapeDtypeStruct((near, piece, depth), jnp.bfloat16),
            jax.ShapeDtypeStruct((far, piece, depth), jnp.bfloat16),
        ),
        in_specs=[VMEM],
        out_specs=(VMEM, VMEM),
        compiler_params=params(),
        name="total",
    )(parts)
    left = lax.all_to_all(to_near, NEAR, 0, 0)
    right = lax.all_to_all(to_far, FAR, 0, 0)
    scale = 1.0 / depth
    block = pl.pallas_call(
        lambda *refs: block_kernel(scale, *refs),
        out_shape=jax.ShapeDtypeStruct((near, far * piece // 2, 128), f32),
        in_specs=[VMEM, VMEM],
        out_specs=VMEM,
        compiler_params=params(),
        name="block",
    )(left, right)
    blocks = lax.all_to_all(block, NEAR, 0, 0)
    return pl.pallas_call(
        lambda *refs: place_kernel(piece, *refs),
        out_shape=jax.ShapeDtypeStruct((rows, far * 128), f32),
        in_specs=[VMEM],
        out_specs=VMEM,
        compiler_params=params(),
        name="place",
    )(blocks)


def solution(mesh):
    fine = Mesh(mesh.devices.reshape(2, 8, 2, 4, 2), ("y_hi", "z", "core", "x", "y_lo"))
    placed = (P(None, None, EAST, NORTH), P(None, EAST, NORTH), P(NORTH, None))
    return jax.shard_map(body, mesh=fine, in_specs=placed, out_specs=P(EAST, None), check_vma=False)
```

```python
import jax
import jax.numpy as jnp
from jax import lax
from jax.experimental import pallas as pl
from jax.experimental.pallas import tpu as pltpu
from jax.sharding import Mesh
from jax.sharding import PartitionSpec as P

VMEM = pl.BlockSpec(memory_space=pltpu.VMEM)
FAR = ("y_hi", "z")
EAST = ("y_hi", "z", "core")
NORTH = ("x", "y_lo")
LIMIT = 48 * 1024 * 1024


def params():
    return pltpu.CompilerParams(vmem_limit_bytes=LIMIT)


def exchanged(value, axes, outer):
    count = lax.axis_size(axes)
    flip = [k ^ 1 for k in range(count)]
    if outer:
        flip = [(k + 1 if k % 2 else k - 1) % count for k in range(count)]
    return lax.ppermute(value, axes, list(enumerate(flip)))


def shifted(value, axes, step):
    count = lax.axis_size(axes)
    return lax.ppermute(value, axes, [(k, (k + step) % count) for k in range(count)])


def faces_kernel(flow, x_inner, x_outer, y_inner, y_outer):
    planes = x_inner.shape[1]
    x_even, y_even = lax.axis_index("core") == 0, lax.axis_index("y_lo") == 0
    lane = lax.broadcasted_iota(jnp.int32, y_inner.shape, 1)
    first = jnp.zeros(y_inner.shape, jnp.float32)
    last = jnp.zeros(y_inner.shape, jnp.float32)
    width = flow.shape[3]
    rows = flow.shape[2]
    for comp in range(3):
        for plane in range(planes):
            top = flow[comp, plane + 2, 0:2, :]
            bottom = flow[comp, plane + 2, rows - 2 : rows, :]
            x_inner[comp, plane] = jnp.where(x_even, bottom, top)
            x_outer[comp, plane] = jnp.where(x_even, top, bottom)
            at = 2 * (comp * planes + plane)
            here = (lane == at) | (lane == at + 1)
            low = flow[comp, plane + 2, :, 0:128]
            high = flow[comp, plane + 2, :, width - 128 : width]
            first = jnp.where(here, pltpu.roll(low, at, 1) if at else low, first)
            last = jnp.where(here, pltpu.roll(high, (at + 2) % 128, 1), last)
    y_inner[...] = jnp.where(y_even, last, first)
    y_outer[...] = jnp.where(y_even, first, last)


def difference(ahead_two, ahead_one, behind_one, behind_two):
    return (8.0 * (ahead_one - behind_one) - (ahead_two - behind_two)) * (1.0 / 12.0)


def inner_kernel(flow, thermal, *refs):
    outs, padded = refs[:7], refs[7]
    planes = thermal.shape[0] - 4
    rows, width = thermal.shape[1], thermal.shape[2]
    total = width + 128
    none = jnp.zeros((rows, 128), jnp.float32)
    padded[:, 0:8, :] = jnp.zeros((3, 8, width), jnp.float32)
    padded[:, 8 + rows :, :] = jnp.zeros((3, 8, width), jnp.float32)
    for plane in range(planes):
        grads = []
        for comp in range(3):
            here = flow[comp, plane + 2]
            along_z = difference(
                flow[comp, plane + 4], flow[comp, plane + 3], flow[comp, plane + 1], flow[comp, plane]
            )
            padded[comp, 8 : 8 + rows, :] = here
            along_x = difference(
                padded[comp, 10 : 10 + rows, :],
                padded[comp, 9 : 9 + rows, :],
                padded[comp, 7 : 7 + rows, :],
                padded[comp, 6 : 6 + rows, :],
            )
            wide = jnp.concatenate([here, none], axis=1)
            along_y = difference(
                pltpu.roll(wide, total - 2, 1)[:, :width],
                pltpu.roll(wide, total - 1, 1)[:, :width],
                pltpu.roll(wide, 1, 1)[:, :width],
                pltpu.roll(wide, 2, 1)[:, :width],
            )
            grads.append((along_z, along_x, along_y))
        outs[0][plane] = grads[0][0]
        outs[1][plane] = grads[1][1]
        outs[2][plane] = grads[2][2]
        outs[3][plane] = grads[0][1] + grads[1][0]
        outs[4][plane] = grads[0][2] + grads[2][0]
        outs[5][plane] = grads[1][2] + grads[2][1]
        outs[6][plane] = 0.1 * jnp.exp(0.7 * jnp.log(thermal[plane + 2]))


def field_kernel(*refs):
    parts, basis = refs[:7], refs[7]
    x_inner, x_outer, y_inner, y_outer, out = refs[8:]
    planes, rows, width = parts[0].shape
    rank = basis.shape[1]
    matrix = basis[...]
    x_even, y_even = lax.axis_index("core") == 0, lax.axis_index("y_lo") == 0
    lane = lax.broadcasted_iota(jnp.int32, (rows, 128), 1)
    even = lane % 2 == 0
    y_low = jnp.where(y_even, y_outer[...], y_inner[...])
    y_high = jnp.where(y_even, y_inner[...], y_outer[...])
    y_low = jnp.where(even, y_low - 8.0 * pltpu.roll(y_low, 127, 1), y_low) * (1.0 / 12.0)
    y_high = jnp.where(even, -y_high, 8.0 * pltpu.roll(y_high, 1, 1) - y_high) * (1.0 / 12.0)
    blank = jnp.zeros((6, width), jnp.float32)

    def with_x(value, comp, plane):
        inner, outer = x_inner[comp, plane], x_outer[comp, plane]
        low = jnp.where(x_even, outer, inner)
        high = jnp.where(x_even, inner, outer)
        head = jnp.concatenate([low[0:1] - 8.0 * low[1:2], low[1:2], blank], axis=0)
        tail = jnp.concatenate([blank, -high[0:1], 8.0 * high[0:1] - high[1:2]], axis=0)
        return jnp.concatenate(
            [value[:8] + head * (1.0 / 12.0), value[8 : rows - 8], value[rows - 8 :] + tail * (1.0 / 12.0)],
            axis=0,
        )

    def with_y(value, comp, plane):
        at = 2 * (comp * planes + plane)
        low = pltpu.roll(y_low, 128 - at, 1) if at else y_low
        high = pltpu.roll(y_high, 126 - at, 1)
        return jnp.concatenate(
            [
                value[:, :128] + jnp.where(lane < 2, low, 0.0),
                        value[:, width - 128 :] + jnp.where(lane >= 126, high, 0.0),
            ],
            axis=1,
        )

    for plane in range(planes):
        along = parts[0][plane]
        down = with_x(parts[1][plane], 1, plane)
        over = with_y(parts[2][plane], 2, plane)
        cross_x = with_x(parts[3][plane], 0, plane)
        cross_y = with_y(parts[4][plane], 0, plane)
        cross_xy = with_x(with_y(parts[5][plane], 1, plane), 2, plane)
        expansion = along + down + over
        rate = (
            2.0 * (along * along + down * down + over * over)
            + (cross_x * cross_x + cross_y * cross_y + cross_xy * cross_xy)
            - (2.0 / 3.0) * (expansion * expansion)
        )
        field = parts[6][plane] * rate
        out[:, plane * rank : (plane + 1) * rank] = jnp.dot(
            field.astype(jnp.bfloat16), matrix, preferred_element_type=jnp.float32
        )


def sum_kernel(parts, own, far):
    total = parts[0]
    for part in range(1, parts.shape[0]):
        total = total + parts[part]
    piece = total.astype(jnp.bfloat16)
    own[0] = piece
    for at in range(far.shape[0]):
        far[at] = piece


def arrange_kernel(*refs):
    pieces, left = refs[:8], refs[8]
    x, y_lo = lax.axis_index("x"), lax.axis_index("y_lo")
    for step in range(4):
        at = 2 * lax.rem(x + step, 4)
        left[at + y_lo] = pieces[step][0]
        left[at + 1 - y_lo] = pieces[4 + step][0]


def block_kernel(scale, left, own, other, out, right):
    core = lax.axis_index("core")
    count, piece, depth = own.shape
    a = left[...].reshape(left.shape[0] * piece, depth)
    half = count // 2
    right[core] = own[...]
    right[1 - core] = other[...]
    sides = []
    for side in range(2):
        w = right[:, side * half : (side + 1) * half].reshape(count * piece, depth)
        sides.append(lax.dot_general(w, a, (((1,), (1,)), ((), ())), preferred_element_type=jnp.float32))
    block = jnp.concatenate(sides, axis=1) * scale
    for at in range(out.shape[0]):
        out[at] = block


def place_kernel(piece, blocks, out):
    count, total, _ = blocks.shape
    tiles = total // (2 * piece)
    side = out.shape[0]
    for tile in range(tiles):
        rows = [
            blocks[at, (core * tiles + tile) * piece : (core * tiles + tile + 1) * piece, :]
            for core in range(2)
            for at in range(count)
        ]
        turned = jnp.concatenate(rows, axis=0).T
        out[:, tile * 128 : (tile + 1) * 128] = turned[:side]
        out[:, (tiles + tile) * 128 : (tiles + tile + 1) * 128] = turned[side:]


def body(flow, thermal, basis):
    planes = thermal.shape[0] - 4
    rows, width = thermal.shape[1], thermal.shape[2]
    rank = basis.shape[1]
    f32 = jnp.float32
    x_face = jax.ShapeDtypeStruct((3, planes, 2, width), f32)
    y_face = jax.ShapeDtypeStruct((rows, 128), f32)
    x_inner, x_outer, y_inner, y_outer = pl.pallas_call(
        faces_kernel,
        out_shape=(x_face, x_face, y_face, y_face),
        in_specs=[VMEM],
        out_specs=(VMEM,) * 4,
        compiler_params=params(),
        name="faces",
    )(flow)
    x_outer = exchanged(x_outer, EAST, True)
    y_outer = exchanged(y_outer, NORTH, True)
    y_inner = exchanged(y_inner, NORTH, False)
    x_inner = exchanged(x_inner, EAST, False)
    parts = pl.pallas_call(
        inner_kernel,
        out_shape=(jax.ShapeDtypeStruct((planes, rows, width), f32),) * 7,
        in_specs=[VMEM, VMEM],
        out_specs=(VMEM,) * 7,
        scratch_shapes=[pltpu.VMEM((3, rows + 16, width), f32)],
        compiler_params=params(),
        cost_estimate=pl.CostEstimate(flops=2_500_000_000, bytes_accessed=5_000_000, transcendentals=0),
        name="inner",
    )(flow, thermal)
    partial = pl.pallas_call(
        field_kernel,
        out_shape=jax.ShapeDtypeStruct((rows, planes * rank), f32),
        in_specs=[VMEM] * 12,
        out_specs=VMEM,
        compiler_params=params(),
        name="field",
    )(*parts, basis, x_inner, x_outer, y_inner, y_outer)
    north = lax.axis_size(NORTH)
    far = lax.axis_size(FAR)
    piece = rows // north
    depth = planes * rank
    gathered = lax.all_to_all(partial.reshape(north, piece, depth), NORTH, 0, 0)
    own, to_far = pl.pallas_call(
        sum_kernel,
        out_shape=(
            jax.ShapeDtypeStruct((1, piece, depth), jnp.bfloat16),
            jax.ShapeDtypeStruct((far, piece, depth), jnp.bfloat16),
        ),
        in_specs=[VMEM],
        out_specs=(VMEM, VMEM),
        compiler_params=params(),
        name="total",
    )(gathered)
    right = lax.all_to_all(to_far, FAR, 0, 0)
    pieces = [own] + [shifted(own, "x", -step) for step in range(1, 4)]
    for step in range(4):
        pairs = [(2 * k + b, 2 * ((k - step) % 4) + 1 - b) for k in range(4) for b in range(2)]
        pieces.append(lax.ppermute(own, NORTH, pairs))
    left = pl.pallas_call(
        arrange_kernel,
        out_shape=jax.ShapeDtypeStruct((north, piece, depth), jnp.bfloat16),
        in_specs=[VMEM] * 8,
        out_specs=VMEM,
        compiler_params=params(),
        cost_estimate=pl.CostEstimate(flops=5_000_000_000, bytes_accessed=4 * piece * depth * north, transcendentals=0),
        name="arrange",
    )(*pieces)
    other = shifted(right, "core", 1)
    scale = 1.0 / depth
    block = pl.pallas_call(
        lambda *refs: block_kernel(scale, *refs),
        out_shape=jax.ShapeDtypeStruct((north, far * piece, 128), f32),
        in_specs=[VMEM] * 3,
        out_specs=VMEM,
        scratch_shapes=[pltpu.VMEM((2, far, piece, depth), jnp.bfloat16)],
        compiler_params=params(),
        name="block",
    )(left, right, other)
    blocks = lax.all_to_all(block, NORTH, 0, 0)
    return pl.pallas_call(
        lambda *refs: place_kernel(piece, *refs),
        out_shape=jax.ShapeDtypeStruct((rows, far * 128), f32),
        in_specs=[VMEM],
        out_specs=VMEM,
        compiler_params=params(),
        name="place",
    )(blocks)


def solution(mesh):
    fine = Mesh(mesh.devices.reshape(2, 8, 2, 4, 2), ("y_hi", "z", "core", "x", "y_lo"))
    placed = (P(None, None, EAST, NORTH), P(None, EAST, NORTH), P(NORTH, None))
    return jax.shard_map(body, mesh=fine, in_specs=placed, out_specs=P(EAST, None), check_vma=False)
```

```python
import jax
import jax.numpy as jnp
from jax import lax
from jax.experimental import pallas as pl
from jax.experimental.pallas import tpu as pltpu
from jax.sharding import Mesh
from jax.sharding import PartitionSpec as P

VMEM = pl.BlockSpec(memory_space=pltpu.VMEM)
FAR = ("y_hi", "z")
EAST = ("y_hi", "z", "core")
NORTH = ("x", "y_lo")
LIMIT = 48 * 1024 * 1024


def params():
    return pltpu.CompilerParams(vmem_limit_bytes=LIMIT)


def exchanged(value, axes, outer):
    count = lax.axis_size(axes)
    flip = [k ^ 1 for k in range(count)]
    if outer:
        flip = [(k + 1 if k % 2 else k - 1) % count for k in range(count)]
    return lax.ppermute(value, axes, list(enumerate(flip)))


def shifted(value, axes, step):
    count = lax.axis_size(axes)
    return lax.ppermute(value, axes, [(k, (k + step) % count) for k in range(count)])


def faces_kernel(flow, x_inner, x_outer, y_inner, y_outer):
    planes = x_inner.shape[1]
    x_even, y_even = lax.axis_index("core") == 0, lax.axis_index("y_lo") == 0
    width = flow.shape[3]
    rows = flow.shape[2]
    lane = lax.broadcasted_iota(jnp.int32, (rows, 128), 1)
    first = jnp.zeros((rows, 128), jnp.float32)
    last = jnp.zeros((rows, 128), jnp.float32)
    for comp in range(3):
        for plane in range(planes):
            top = flow[comp, plane + 2, 0:2, :]
            bottom = flow[comp, plane + 2, rows - 2 : rows, :]
            x_inner[comp, plane] = jnp.where(x_even, bottom, top)
            x_outer[comp, plane] = jnp.where(x_even, top, bottom)
            at = 2 * (comp * planes + plane)
            here = (lane == at) | (lane == at + 1)
            low = flow[comp, plane + 2, :, 0:128]
            high = flow[comp, plane + 2, :, width - 128 : width]
            first = jnp.where(here, pltpu.roll(low, at, 1) if at else low, first)
            last = jnp.where(here, pltpu.roll(high, (at + 2) % 128, 1), last)
    y_inner[:rows] = jnp.where(y_even, last, first)
    y_outer[:rows] = jnp.where(y_even, first, last)


def difference(ahead_two, ahead_one, behind_one, behind_two):
    return (8.0 * (ahead_one - behind_one) - (ahead_two - behind_two)) * (1.0 / 12.0)


def inner_kernel(flow, thermal, *refs):
    outs, padded = refs[:7], refs[7]
    planes = thermal.shape[0] - 4
    rows, width = thermal.shape[1], thermal.shape[2]
    total = width + 128
    none = jnp.zeros((rows, 128), jnp.float32)
    padded[:, 0:8, :] = jnp.zeros((3, 8, width), jnp.float32)
    padded[:, 8 + rows :, :] = jnp.zeros((3, 8, width), jnp.float32)
    for plane in range(planes):
        grads = []
        for comp in range(3):
            here = flow[comp, plane + 2]
            along_z = difference(
                flow[comp, plane + 4], flow[comp, plane + 3], flow[comp, plane + 1], flow[comp, plane]
            )
            padded[comp, 8 : 8 + rows, :] = here
            along_x = difference(
                padded[comp, 10 : 10 + rows, :],
                padded[comp, 9 : 9 + rows, :],
                padded[comp, 7 : 7 + rows, :],
                padded[comp, 6 : 6 + rows, :],
            )
            wide = jnp.concatenate([here, none], axis=1)
            along_y = difference(
                pltpu.roll(wide, total - 2, 1)[:, :width],
                pltpu.roll(wide, total - 1, 1)[:, :width],
                pltpu.roll(wide, 1, 1)[:, :width],
                pltpu.roll(wide, 2, 1)[:, :width],
            )
            grads.append((along_z, along_x, along_y))
        outs[0][plane] = grads[0][0]
        outs[1][plane] = grads[1][1]
        outs[2][plane] = grads[2][2]
        outs[3][plane] = grads[0][1] + grads[1][0]
        outs[4][plane] = grads[0][2] + grads[2][0]
        outs[5][plane] = grads[1][2] + grads[2][1]
        outs[6][plane] = 0.1 * jnp.exp(0.7 * jnp.log(thermal[plane + 2]))


def field_kernel(*refs):
    parts, basis = refs[:7], refs[7]
    x_outer, y_outer, y_inner, x_inner, out = refs[8:]
    planes, rows, width = parts[0].shape
    rank = basis.shape[1]
    matrix = basis[...]
    x_even, y_even = lax.axis_index("core") == 0, lax.axis_index("y_lo") == 0
    lane = lax.broadcasted_iota(jnp.int32, (rows, 128), 1)
    even = lane % 2 == 0
    y_low = jnp.where(y_even, y_outer[:rows], y_inner[:rows])
    y_high = jnp.where(y_even, y_inner[:rows], y_outer[:rows])
    y_low = jnp.where(even, y_low - 8.0 * pltpu.roll(y_low, 127, 1), y_low) * (1.0 / 12.0)
    y_high = jnp.where(even, -y_high, 8.0 * pltpu.roll(y_high, 1, 1) - y_high) * (1.0 / 12.0)
    blank = jnp.zeros((6, width), jnp.float32)

    def with_x(value, comp, plane):
        inner, outer = x_inner[comp, plane], x_outer[comp, plane]
        low = jnp.where(x_even, outer, inner)
        high = jnp.where(x_even, inner, outer)
        head = jnp.concatenate([low[0:1] - 8.0 * low[1:2], low[1:2], blank], axis=0)
        tail = jnp.concatenate([blank, -high[0:1], 8.0 * high[0:1] - high[1:2]], axis=0)
        return jnp.concatenate(
            [value[:8] + head * (1.0 / 12.0), value[8 : rows - 8], value[rows - 8 :] + tail * (1.0 / 12.0)],
            axis=0,
        )

    def with_y(value, comp, plane):
        at = 2 * (comp * planes + plane)
        low = pltpu.roll(y_low, 128 - at, 1) if at else y_low
        high = pltpu.roll(y_high, 126 - at, 1)
        return jnp.concatenate(
            [
                value[:, :128] + jnp.where(lane < 2, low, 0.0),
                        value[:, width - 128 :] + jnp.where(lane >= 126, high, 0.0),
            ],
            axis=1,
        )

    for plane in range(planes):
        along = parts[0][plane]
        down = with_x(parts[1][plane], 1, plane)
        over = with_y(parts[2][plane], 2, plane)
        cross_x = with_x(parts[3][plane], 0, plane)
        cross_y = with_y(parts[4][plane], 0, plane)
        cross_xy = with_x(with_y(parts[5][plane], 1, plane), 2, plane)
        expansion = along + down + over
        rate = (
            2.0 * (along * along + down * down + over * over)
            + (cross_x * cross_x + cross_y * cross_y + cross_xy * cross_xy)
            - (2.0 / 3.0) * (expansion * expansion)
        )
        field = parts[6][plane] * rate
        out[:, plane * rank : (plane + 1) * rank] = jnp.dot(
            field.astype(jnp.bfloat16), matrix, preferred_element_type=jnp.float32
        )


def sum_kernel(parts, own, far):
    total = parts[0]
    for part in range(1, parts.shape[0]):
        total = total + parts[part]
    piece = total.astype(jnp.bfloat16)
    own[0] = piece
    for at in range(far.shape[0]):
        far[at] = piece


def copy_kernel(source, target):
    target[...] = source[...]


def arrange_kernel(near, across, left):
    x, y_lo = lax.axis_index("x"), lax.axis_index("y_lo")
    for step in range(4):
        at = 2 * lax.rem(x + step, 4)
        left[at + y_lo] = near[step]
        left[at + 1 - y_lo] = across[step]


def block_kernel(scale, left, own, other, out, right):
    core = lax.axis_index("core")
    count, piece, depth = own.shape
    a = left[...].reshape(left.shape[0] * piece, depth)
    half = count // 2
    right[core] = own[...]
    right[1 - core] = other[...]
    sides = []
    for side in range(2):
        w = right[:, side * half : (side + 1) * half].reshape(count * piece, depth)
        sides.append(lax.dot_general(w, a, (((1,), (1,)), ((), ())), preferred_element_type=jnp.float32))
    block = jnp.concatenate(sides, axis=1) * scale
    for at in range(out.shape[0]):
        out[at] = block


def place_kernel(piece, blocks, out):
    count, total, _ = blocks.shape
    tiles = total // (2 * piece)
    side = out.shape[0]
    for tile in range(tiles):
        rows = [
            blocks[at, (core * tiles + tile) * piece : (core * tiles + tile + 1) * piece, :]
            for core in range(2)
            for at in range(count)
        ]
        turned = jnp.concatenate(rows, axis=0).T
        out[:, tile * 128 : (tile + 1) * 128] = turned[:side]
        out[:, (tiles + tile) * 128 : (tiles + tile + 1) * 128] = turned[side:]


def body(flow, thermal, basis):
    planes = thermal.shape[0] - 4
    rows, width = thermal.shape[1], thermal.shape[2]
    rank = basis.shape[1]
    f32 = jnp.float32
    x_face = jax.ShapeDtypeStruct((3, planes, 2, width), f32)
    y_face = jax.ShapeDtypeStruct((rows + 16, 128), f32)
    x_inner, x_outer, y_inner, y_outer = pl.pallas_call(
        faces_kernel,
        out_shape=(x_face, x_face, y_face, y_face),
        in_specs=[VMEM],
        out_specs=(VMEM,) * 4,
        compiler_params=params(),
        name="faces",
    )(flow)
    x_outer = exchanged(x_outer, EAST, True)
    y_outer = exchanged(y_outer, NORTH, True)
    y_inner = exchanged(y_inner, NORTH, False)
    x_inner = exchanged(x_inner, EAST, False)
    parts = pl.pallas_call(
        inner_kernel,
        out_shape=(jax.ShapeDtypeStruct((planes, rows, width), f32),) * 7,
        in_specs=[VMEM, VMEM],
        out_specs=(VMEM,) * 7,
        scratch_shapes=[pltpu.VMEM((3, rows + 16, width), f32)],
        compiler_params=params(),
        cost_estimate=pl.CostEstimate(flops=2_500_000_000, bytes_accessed=5_000_000, transcendentals=0),
        name="inner",
    )(flow, thermal)
    partial = pl.pallas_call(
        field_kernel,
        out_shape=jax.ShapeDtypeStruct((rows, planes * rank), f32),
        in_specs=[VMEM] * 12,
        out_specs=VMEM,
        compiler_params=params(),
        name="field",
    )(*parts, basis, x_outer, y_outer, y_inner, x_inner)
    north = lax.axis_size(NORTH)
    far = lax.axis_size(FAR)
    piece = rows // north
    depth = planes * rank
    gathered = lax.all_to_all(partial.reshape(north, piece, depth), NORTH, 0, 0)
    own, to_far = pl.pallas_call(
        sum_kernel,
        out_shape=(
            jax.ShapeDtypeStruct((1, piece, depth), jnp.bfloat16),
            jax.ShapeDtypeStruct((far, piece, depth), jnp.bfloat16),
        ),
        in_specs=[VMEM],
        out_specs=(VMEM, VMEM),
        compiler_params=params(),
        name="total",
    )(gathered)
    right = lax.all_to_all(to_far, FAR, 0, 0)
    own = pl.pallas_call(
        copy_kernel,
        out_shape=jax.ShapeDtypeStruct(own.shape, own.dtype),
        in_specs=[VMEM],
        out_specs=VMEM,
        compiler_params=params(),
        cost_estimate=pl.CostEstimate(flops=10_000_000_000, bytes_accessed=4 * piece * depth, transcendentals=0),
        name="own",
    )(own)
    near = jnp.concatenate([own] + [shifted(own, "x", -step) for step in range(1, 4)])
    across = shifted(near, "y_lo", 1)
    left = pl.pallas_call(
        arrange_kernel,
        out_shape=jax.ShapeDtypeStruct((north, piece, depth), jnp.bfloat16),
        in_specs=[VMEM] * 2,
        out_specs=VMEM,
        compiler_params=params(),
        cost_estimate=pl.CostEstimate(flops=5_000_000_000, bytes_accessed=4 * piece * depth * north, transcendentals=0),
        name="arrange",
    )(near, across)
    other = shifted(right, "core", 1)
    scale = 1.0 / depth
    block = pl.pallas_call(
        lambda *refs: block_kernel(scale, *refs),
        out_shape=jax.ShapeDtypeStruct((north, far * piece, 128), f32),
        in_specs=[VMEM] * 3,
        out_specs=VMEM,
        scratch_shapes=[pltpu.VMEM((2, far, piece, depth), jnp.bfloat16)],
        compiler_params=params(),
        name="block",
    )(left, right, other)
    blocks = lax.all_to_all(block, NORTH, 0, 0)
    return pl.pallas_call(
        lambda *refs: place_kernel(piece, *refs),
        out_shape=jax.ShapeDtypeStruct((rows, far * 128), f32),
        in_specs=[VMEM],
        out_specs=VMEM,
        compiler_params=params(),
        name="place",
    )(blocks)


def solution(mesh):
    fine = Mesh(mesh.devices.reshape(2, 8, 2, 4, 2), ("y_hi", "z", "core", "x", "y_lo"))
    placed = (P(None, None, EAST, NORTH), P(None, EAST, NORTH), P(NORTH, None))
    return jax.shard_map(body, mesh=fine, in_specs=placed, out_specs=P(EAST, None), check_vma=False)
```

```python
import jax
import jax.numpy as jnp
from jax import lax
from jax.experimental import pallas as pl
from jax.experimental.pallas import tpu as pltpu
from jax.sharding import Mesh
from jax.sharding import PartitionSpec as P

VMEM = pl.BlockSpec(memory_space=pltpu.VMEM)
FAR = ("y_hi", "z")
EAST = ("y_hi", "z", "core")
NORTH = ("x", "y_lo")
LIMIT = 48 * 1024 * 1024


def params():
    return pltpu.CompilerParams(vmem_limit_bytes=LIMIT)


def exchanged(value, axes, outer):
    count = lax.axis_size(axes)
    flip = [k ^ 1 for k in range(count)]
    if outer:
        flip = [(k + 1 if k % 2 else k - 1) % count for k in range(count)]
    return lax.ppermute(value, axes, list(enumerate(flip)))


def shifted(value, axes, step):
    count = lax.axis_size(axes)
    return lax.ppermute(value, axes, [(k, (k + step) % count) for k in range(count)])


def x_faces_kernel(flow, x_inner, x_outer, top, bottom, sems):
    planes, rows = x_inner.shape[1], flow.shape[2]
    middle = slice(2, planes + 2)
    copies = [
        pltpu.make_async_copy(flow.at[:, middle, 0:8], top, sems.at[0]),
        pltpu.make_async_copy(flow.at[:, middle, rows - 8 : rows], bottom, sems.at[1]),
    ]
    for copy in copies:
        copy.start()
    for copy in copies:
        copy.wait()
    x_even = lax.axis_index("core") == 0
    for comp in range(3):
        for plane in range(planes):
            first, last = top[comp, plane, 0:2], bottom[comp, plane, 6:8]
            x_inner[comp, plane] = jnp.where(x_even, last, first)
            x_outer[comp, plane] = jnp.where(x_even, first, last)


def y_faces_kernel(flow, y_inner, y_outer):
    planes, rows, width = flow.shape[1] - 4, flow.shape[2], flow.shape[3]
    y_even = lax.axis_index("y_lo") == 0
    lane = lax.broadcasted_iota(jnp.int32, (rows, 128), 1)
    first = jnp.zeros((rows, 128), jnp.float32)
    last = jnp.zeros((rows, 128), jnp.float32)
    for comp in range(3):
        for plane in range(planes):
            at = 2 * (comp * planes + plane)
            here = (lane == at) | (lane == at + 1)
            low = flow[comp, plane + 2, :, 0:128]
            high = flow[comp, plane + 2, :, width - 128 : width]
            first = jnp.where(here, pltpu.roll(low, at, 1) if at else low, first)
            last = jnp.where(here, pltpu.roll(high, (at + 2) % 128, 1), last)
    y_inner[:rows] = jnp.where(y_even, last, first)
    y_outer[:rows] = jnp.where(y_even, first, last)


def difference(ahead_two, ahead_one, behind_one, behind_two):
    return (8.0 * (ahead_one - behind_one) - (ahead_two - behind_two)) * (1.0 / 12.0)


def inner_kernel(flow, thermal, *refs):
    outs, padded = refs[:7], refs[7]
    planes = thermal.shape[0] - 4
    rows, width = thermal.shape[1], thermal.shape[2]
    total = width + 128
    none = jnp.zeros((rows, 128), jnp.float32)
    padded[:, 0:8, :] = jnp.zeros((3, 8, width), jnp.float32)
    padded[:, 8 + rows :, :] = jnp.zeros((3, 8, width), jnp.float32)
    for plane in range(planes):
        grads = []
        for comp in range(3):
            here = flow[comp, plane + 2]
            along_z = difference(
                flow[comp, plane + 4], flow[comp, plane + 3], flow[comp, plane + 1], flow[comp, plane]
            )
            padded[comp, 8 : 8 + rows, :] = here
            along_x = difference(
                padded[comp, 10 : 10 + rows, :],
                padded[comp, 9 : 9 + rows, :],
                padded[comp, 7 : 7 + rows, :],
                padded[comp, 6 : 6 + rows, :],
            )
            wide = jnp.concatenate([here, none], axis=1)
            along_y = difference(
                pltpu.roll(wide, total - 2, 1)[:, :width],
                pltpu.roll(wide, total - 1, 1)[:, :width],
                pltpu.roll(wide, 1, 1)[:, :width],
                pltpu.roll(wide, 2, 1)[:, :width],
            )
            grads.append((along_z, along_x, along_y))
        outs[0][plane] = grads[0][0]
        outs[1][plane] = grads[1][1]
        outs[2][plane] = grads[2][2]
        outs[3][plane] = grads[0][1] + grads[1][0]
        outs[4][plane] = grads[0][2] + grads[2][0]
        outs[5][plane] = grads[1][2] + grads[2][1]
        outs[6][plane] = 0.1 * jnp.exp(0.7 * jnp.log(thermal[plane + 2]))


def field_kernel(*refs):
    parts, basis = refs[:7], refs[7]
    x_outer, y_outer, y_inner, x_inner, out = refs[8:]
    planes, rows, width = parts[0].shape
    rank = basis.shape[1]
    matrix = basis[...]
    x_even, y_even = lax.axis_index("core") == 0, lax.axis_index("y_lo") == 0
    lane = lax.broadcasted_iota(jnp.int32, (rows, 128), 1)
    even = lane % 2 == 0
    y_low = jnp.where(y_even, y_outer[:rows], y_inner[:rows])
    y_high = jnp.where(y_even, y_inner[:rows], y_outer[:rows])
    y_low = jnp.where(even, y_low - 8.0 * pltpu.roll(y_low, 127, 1), y_low) * (1.0 / 12.0)
    y_high = jnp.where(even, -y_high, 8.0 * pltpu.roll(y_high, 1, 1) - y_high) * (1.0 / 12.0)
    blank = jnp.zeros((6, width), jnp.float32)

    def with_x(value, comp, plane):
        inner, outer = x_inner[comp, plane], x_outer[comp, plane]
        low = jnp.where(x_even, outer, inner)
        high = jnp.where(x_even, inner, outer)
        head = jnp.concatenate([low[0:1] - 8.0 * low[1:2], low[1:2], blank], axis=0)
        tail = jnp.concatenate([blank, -high[0:1], 8.0 * high[0:1] - high[1:2]], axis=0)
        return jnp.concatenate(
            [value[:8] + head * (1.0 / 12.0), value[8 : rows - 8], value[rows - 8 :] + tail * (1.0 / 12.0)],
            axis=0,
        )

    def with_y(value, comp, plane):
        at = 2 * (comp * planes + plane)
        low = pltpu.roll(y_low, 128 - at, 1) if at else y_low
        high = pltpu.roll(y_high, 126 - at, 1)
        return jnp.concatenate(
            [
                value[:, :128] + jnp.where(lane < 2, low, 0.0),
                        value[:, width - 128 :] + jnp.where(lane >= 126, high, 0.0),
            ],
            axis=1,
        )

    for plane in range(planes):
        along = parts[0][plane]
        down = with_x(parts[1][plane], 1, plane)
        over = with_y(parts[2][plane], 2, plane)
        cross_x = with_x(parts[3][plane], 0, plane)
        cross_y = with_y(parts[4][plane], 0, plane)
        cross_xy = with_x(with_y(parts[5][plane], 1, plane), 2, plane)
        expansion = along + down + over
        rate = (
            2.0 * (along * along + down * down + over * over)
            + (cross_x * cross_x + cross_y * cross_y + cross_xy * cross_xy)
            - (2.0 / 3.0) * (expansion * expansion)
        )
        field = parts[6][plane] * rate
        out[:, plane * rank : (plane + 1) * rank] = jnp.dot(
            field.astype(jnp.bfloat16), matrix, preferred_element_type=jnp.float32
        )


def sum_kernel(parts, own, far):
    total = parts[0]
    for part in range(1, parts.shape[0]):
        total = total + parts[part]
    piece = total.astype(jnp.bfloat16)
    own[0] = piece
    for at in range(far.shape[0]):
        far[at] = piece


def copy_kernel(source, target):
    target[...] = source[...]


def arrange_kernel(near, across, left):
    x, y_lo = lax.axis_index("x"), lax.axis_index("y_lo")
    for step in range(4):
        at = 2 * lax.rem(x + step, 4)
        left[at + y_lo] = near[step]
        left[at + 1 - y_lo] = across[step]


def block_kernel(scale, left, own, other, out, right):
    core = lax.axis_index("core")
    count, piece, depth = own.shape
    a = left[...].reshape(left.shape[0] * piece, depth)
    half = count // 2
    right[core] = own[...]
    right[1 - core] = other[...]
    sides = []
    for side in range(2):
        w = right[:, side * half : (side + 1) * half].reshape(count * piece, depth)
        sides.append(lax.dot_general(w, a, (((1,), (1,)), ((), ())), preferred_element_type=jnp.float32))
    block = jnp.concatenate(sides, axis=1) * scale
    for at in range(out.shape[0]):
        out[at] = block


def place_kernel(piece, blocks, out):
    count, total, _ = blocks.shape
    tiles = total // (2 * piece)
    side = out.shape[0]
    for tile in range(tiles):
        rows = [
            blocks[at, (core * tiles + tile) * piece : (core * tiles + tile + 1) * piece, :]
            for core in range(2)
            for at in range(count)
        ]
        turned = jnp.concatenate(rows, axis=0).T
        out[:, tile * 128 : (tile + 1) * 128] = turned[:side]
        out[:, (tiles + tile) * 128 : (tiles + tile + 1) * 128] = turned[side:]


def body(flow, thermal, basis):
    planes = thermal.shape[0] - 4
    rows, width = thermal.shape[1], thermal.shape[2]
    rank = basis.shape[1]
    f32 = jnp.float32
    x_face = jax.ShapeDtypeStruct((3, planes, 2, width), f32)
    y_face = jax.ShapeDtypeStruct((rows + 16, 128), f32)
    x_inner, x_outer = pl.pallas_call(
        x_faces_kernel,
        out_shape=(x_face, x_face),
        in_specs=[pl.BlockSpec(memory_space=pltpu.HBM)],
        out_specs=(VMEM, VMEM),
        scratch_shapes=[
            pltpu.VMEM((3, planes, 8, width), f32),
            pltpu.VMEM((3, planes, 8, width), f32),
            pltpu.SemaphoreType.DMA((2,)),
        ],
        compiler_params=params(),
        name="x_faces",
    )(flow)
    y_inner, y_outer = pl.pallas_call(
        y_faces_kernel,
        out_shape=(y_face, y_face),
        in_specs=[VMEM],
        out_specs=(VMEM, VMEM),
        compiler_params=params(),
        cost_estimate=pl.CostEstimate(flops=500_000_000, bytes_accessed=1_000_000, transcendentals=0),
        name="y_faces",
    )(flow)
    x_outer = exchanged(x_outer, EAST, True)
    y_outer = exchanged(y_outer, NORTH, True)
    y_inner = exchanged(y_inner, NORTH, False)
    x_inner = exchanged(x_inner, EAST, False)
    parts = pl.pallas_call(
        inner_kernel,
        out_shape=(jax.ShapeDtypeStruct((planes, rows, width), f32),) * 7,
        in_specs=[VMEM, VMEM],
        out_specs=(VMEM,) * 7,
        scratch_shapes=[pltpu.VMEM((3, rows + 16, width), f32)],
        compiler_params=params(),
        cost_estimate=pl.CostEstimate(flops=2_500_000_000, bytes_accessed=5_000_000, transcendentals=0),
        name="inner",
    )(flow, thermal)
    partial = pl.pallas_call(
        field_kernel,
        out_shape=jax.ShapeDtypeStruct((rows, planes * rank), f32),
        in_specs=[VMEM] * 12,
        out_specs=VMEM,
        compiler_params=params(),
        name="field",
    )(*parts, basis, x_outer, y_outer, y_inner, x_inner)
    north = lax.axis_size(NORTH)
    far = lax.axis_size(FAR)
    piece = rows // north
    depth = planes * rank
    gathered = lax.all_to_all(partial.reshape(north, piece, depth), NORTH, 0, 0)
    own, to_far = pl.pallas_call(
        sum_kernel,
        out_shape=(
            jax.ShapeDtypeStruct((1, piece, depth), jnp.bfloat16),
            jax.ShapeDtypeStruct((far, piece, depth), jnp.bfloat16),
        ),
        in_specs=[VMEM],
        out_specs=(VMEM, VMEM),
        compiler_params=params(),
        name="total",
    )(gathered)
    right = lax.all_to_all(to_far, FAR, 0, 0)
    own = pl.pallas_call(
        copy_kernel,
        out_shape=jax.ShapeDtypeStruct(own.shape, own.dtype),
        in_specs=[VMEM],
        out_specs=VMEM,
        compiler_params=params(),
        cost_estimate=pl.CostEstimate(flops=10_000_000_000, bytes_accessed=4 * piece * depth, transcendentals=0),
        name="own",
    )(own)
    near = jnp.concatenate([own] + [shifted(own, "x", -step) for step in range(1, 4)])
    across = shifted(near, "y_lo", 1)
    left = pl.pallas_call(
        arrange_kernel,
        out_shape=jax.ShapeDtypeStruct((north, piece, depth), jnp.bfloat16),
        in_specs=[VMEM] * 2,
        out_specs=VMEM,
        compiler_params=params(),
        cost_estimate=pl.CostEstimate(flops=5_000_000_000, bytes_accessed=4 * piece * depth * north, transcendentals=0),
        name="arrange",
    )(near, across)
    other = shifted(right, "core", 1)
    scale = 1.0 / depth
    block = pl.pallas_call(
        lambda *refs: block_kernel(scale, *refs),
        out_shape=jax.ShapeDtypeStruct((north, far * piece, 128), f32),
        in_specs=[VMEM] * 3,
        out_specs=VMEM,
        scratch_shapes=[pltpu.VMEM((2, far, piece, depth), jnp.bfloat16)],
        compiler_params=params(),
        name="block",
    )(left, right, other)
    blocks = lax.all_to_all(block, NORTH, 0, 0)
    return pl.pallas_call(
        lambda *refs: place_kernel(piece, *refs),
        out_shape=jax.ShapeDtypeStruct((rows, far * 128), f32),
        in_specs=[VMEM],
        out_specs=VMEM,
        compiler_params=params(),
        name="place",
    )(blocks)


def solution(mesh):
    fine = Mesh(mesh.devices.reshape(2, 8, 2, 4, 2), ("y_hi", "z", "core", "x", "y_lo"))
    placed = (P(None, None, EAST, NORTH), P(None, EAST, NORTH), P(NORTH, None))
    return jax.shard_map(body, mesh=fine, in_specs=placed, out_specs=P(EAST, None), check_vma=False)
```

```python
import jax
import jax.numpy as jnp
from jax import lax
from jax.experimental import pallas as pl
from jax.experimental.pallas import tpu as pltpu
from jax.sharding import Mesh
from jax.sharding import PartitionSpec as P

VMEM = pl.BlockSpec(memory_space=pltpu.VMEM)
FAR = ("y_hi", "z")
EAST = ("y_hi", "z", "core")
NORTH = ("x", "y_lo")
LIMIT = 48 * 1024 * 1024


def params():
    return pltpu.CompilerParams(vmem_limit_bytes=LIMIT)


def exchanged(value, axes, outer):
    count = lax.axis_size(axes)
    flip = [k ^ 1 for k in range(count)]
    if outer:
        flip = [(k + 1 if k % 2 else k - 1) % count for k in range(count)]
    return lax.ppermute(value, axes, list(enumerate(flip)))


def shifted(value, axes, step):
    count = lax.axis_size(axes)
    return lax.ppermute(value, axes, [(k, (k + step) % count) for k in range(count)])


def x_faces_kernel(flow, x_inner, x_outer, top, bottom, sems):
    planes, rows = x_inner.shape[1], flow.shape[2]
    middle = slice(2, planes + 2)
    copies = [
        pltpu.make_async_copy(flow.at[:, middle, 0:8], top, sems.at[0]),
        pltpu.make_async_copy(flow.at[:, middle, rows - 8 : rows], bottom, sems.at[1]),
    ]
    for copy in copies:
        copy.start()
    for copy in copies:
        copy.wait()
    x_even = lax.axis_index("core") == 0
    for comp in range(3):
        for plane in range(planes):
            first, last = top[comp, plane, 0:2], bottom[comp, plane, 6:8]
            x_inner[comp, plane] = jnp.where(x_even, last, first)
            x_outer[comp, plane] = jnp.where(x_even, first, last)


def y_faces_kernel(flow, y_inner, y_outer):
    planes, rows, width = flow.shape[1] - 4, flow.shape[2], flow.shape[3]
    y_even = lax.axis_index("y_lo") == 0
    lane = lax.broadcasted_iota(jnp.int32, (rows, 128), 1)
    first = jnp.zeros((rows, 128), jnp.float32)
    last = jnp.zeros((rows, 128), jnp.float32)
    for comp in range(3):
        for plane in range(planes):
            at = 2 * (comp * planes + plane)
            here = (lane == at) | (lane == at + 1)
            low = flow[comp, plane + 2, :, 0:128]
            high = flow[comp, plane + 2, :, width - 128 : width]
            first = jnp.where(here, pltpu.roll(low, at, 1) if at else low, first)
            last = jnp.where(here, pltpu.roll(high, (at + 2) % 128, 1), last)
    y_inner[:rows] = jnp.where(y_even, last, first)
    y_outer[:rows] = jnp.where(y_even, first, last)


def difference(ahead_two, ahead_one, behind_one, behind_two):
    return (8.0 * (ahead_one - behind_one) - (ahead_two - behind_two)) * (1.0 / 12.0)


def inner_kernel(flow, thermal, *refs):
    outs, padded = refs[:7], refs[7]
    planes = thermal.shape[0] - 4
    rows, width = thermal.shape[1], thermal.shape[2]
    total = width + 128
    none = jnp.zeros((rows, 128), jnp.float32)
    padded[:, 0:8, :] = jnp.zeros((3, 8, width), jnp.float32)
    padded[:, 8 + rows :, :] = jnp.zeros((3, 8, width), jnp.float32)
    for plane in range(planes):
        grads = []
        for comp in range(3):
            here = flow[comp, plane + 2]
            along_z = difference(
                flow[comp, plane + 4], flow[comp, plane + 3], flow[comp, plane + 1], flow[comp, plane]
            )
            padded[comp, 8 : 8 + rows, :] = here
            along_x = difference(
                padded[comp, 10 : 10 + rows, :],
                padded[comp, 9 : 9 + rows, :],
                padded[comp, 7 : 7 + rows, :],
                padded[comp, 6 : 6 + rows, :],
            )
            wide = jnp.concatenate([here, none], axis=1)
            along_y = difference(
                pltpu.roll(wide, total - 2, 1)[:, :width],
                pltpu.roll(wide, total - 1, 1)[:, :width],
                pltpu.roll(wide, 1, 1)[:, :width],
                pltpu.roll(wide, 2, 1)[:, :width],
            )
            grads.append((along_z, along_x, along_y))
        outs[0][plane] = grads[0][0]
        outs[1][plane] = grads[1][1]
        outs[2][plane] = grads[2][2]
        outs[3][plane] = grads[0][1] + grads[1][0]
        outs[4][plane] = grads[0][2] + grads[2][0]
        outs[5][plane] = grads[1][2] + grads[2][1]
        outs[6][plane] = 0.1 * jnp.exp(0.7 * jnp.log(thermal[plane + 2]))


def field_kernel(*refs):
    parts, basis = refs[:7], refs[7]
    x_outer, y_outer, y_inner, x_inner, out = refs[8:]
    planes, rows, width = parts[0].shape
    rank = basis.shape[1]
    matrix = basis[...]
    x_even, y_even = lax.axis_index("core") == 0, lax.axis_index("y_lo") == 0
    lane = lax.broadcasted_iota(jnp.int32, (rows, 128), 1)
    even = lane % 2 == 0
    y_low = jnp.where(y_even, y_outer[:rows], y_inner[:rows])
    y_high = jnp.where(y_even, y_inner[:rows], y_outer[:rows])
    y_low = jnp.where(even, y_low - 8.0 * pltpu.roll(y_low, 127, 1), y_low) * (1.0 / 12.0)
    y_high = jnp.where(even, -y_high, 8.0 * pltpu.roll(y_high, 1, 1) - y_high) * (1.0 / 12.0)
    blank = jnp.zeros((6, width), jnp.float32)

    def with_x(value, comp, plane):
        inner, outer = x_inner[comp, plane], x_outer[comp, plane]
        low = jnp.where(x_even, outer, inner)
        high = jnp.where(x_even, inner, outer)
        head = jnp.concatenate([low[0:1] - 8.0 * low[1:2], low[1:2], blank], axis=0)
        tail = jnp.concatenate([blank, -high[0:1], 8.0 * high[0:1] - high[1:2]], axis=0)
        return jnp.concatenate(
            [value[:8] + head * (1.0 / 12.0), value[8 : rows - 8], value[rows - 8 :] + tail * (1.0 / 12.0)],
            axis=0,
        )

    def with_y(value, comp, plane):
        at = 2 * (comp * planes + plane)
        low = pltpu.roll(y_low, 128 - at, 1) if at else y_low
        high = pltpu.roll(y_high, 126 - at, 1)
        return jnp.concatenate(
            [
                value[:, :128] + jnp.where(lane < 2, low, 0.0),
                        value[:, width - 128 :] + jnp.where(lane >= 126, high, 0.0),
            ],
            axis=1,
        )

    for plane in range(planes):
        along = parts[0][plane]
        down = with_x(parts[1][plane], 1, plane)
        over = with_y(parts[2][plane], 2, plane)
        cross_x = with_x(parts[3][plane], 0, plane)
        cross_y = with_y(parts[4][plane], 0, plane)
        cross_xy = with_x(with_y(parts[5][plane], 1, plane), 2, plane)
        expansion = along + down + over
        rate = (
            2.0 * (along * along + down * down + over * over)
            + (cross_x * cross_x + cross_y * cross_y + cross_xy * cross_xy)
            - (2.0 / 3.0) * (expansion * expansion)
        )
        field = parts[6][plane] * rate
        out[:, plane * rank : (plane + 1) * rank] = jnp.dot(
            field.astype(jnp.bfloat16), matrix, preferred_element_type=jnp.float32
        )


def sum_kernel(parts, own, far):
    total = parts[0]
    for part in range(1, parts.shape[0]):
        total = total + parts[part]
    piece = total.astype(jnp.bfloat16)
    own[0] = piece
    for at in range(far.shape[0]):
        far[at] = piece


def copy_kernel(source, target):
    target[...] = source[...]


def arrange_kernel(near, across, left):
    x, y_lo = lax.axis_index("x"), lax.axis_index("y_lo")
    for step in range(4):
        at = 2 * lax.rem(x + step, 4)
        left[at + y_lo] = near[step]
        left[at + 1 - y_lo] = across[step]


def block_kernel(scale, left, own, other, out, right):
    core = lax.axis_index("core")
    count, piece, depth = own.shape
    a = left[...].reshape(left.shape[0] * piece, depth)
    half = count // 2
    right[core] = own[...]
    right[1 - core] = other[...]
    sides = []
    for side in range(2):
        w = right[:, side * half : (side + 1) * half].reshape(count * piece, depth)
        sides.append(lax.dot_general(w, a, (((1,), (1,)), ((), ())), preferred_element_type=jnp.float32))
    block = jnp.concatenate(sides, axis=1) * scale
    for at in range(out.shape[0]):
        out[at] = block


def place_kernel(piece, blocks, out):
    count, total, _ = blocks.shape
    tiles = total // (2 * piece)
    side = out.shape[0]
    for tile in range(tiles):
        rows = [
            blocks[at, (core * tiles + tile) * piece : (core * tiles + tile + 1) * piece, :]
            for core in range(2)
            for at in range(count)
        ]
        turned = jnp.concatenate(rows, axis=0).T
        out[:, tile * 128 : (tile + 1) * 128] = turned[:side]
        out[:, (tiles + tile) * 128 : (tiles + tile + 1) * 128] = turned[side:]


def body(flow, thermal, basis):
    planes = thermal.shape[0] - 4
    rows, width = thermal.shape[1], thermal.shape[2]
    rank = basis.shape[1]
    f32 = jnp.float32
    x_face = jax.ShapeDtypeStruct((3, planes, 2, width), f32)
    y_face = jax.ShapeDtypeStruct((rows + 16, 128), f32)
    x_inner, x_outer = pl.pallas_call(
        x_faces_kernel,
        out_shape=(x_face, x_face),
        in_specs=[pl.BlockSpec(memory_space=pltpu.HBM)],
        out_specs=(VMEM, VMEM),
        scratch_shapes=[
            pltpu.VMEM((3, planes, 8, width), f32),
            pltpu.VMEM((3, planes, 8, width), f32),
            pltpu.SemaphoreType.DMA((2,)),
        ],
        compiler_params=params(),
        name="x_faces",
    )(pltpu.with_memory_space_constraint(flow, pltpu.HBM))
    y_inner, y_outer = pl.pallas_call(
        y_faces_kernel,
        out_shape=(y_face, y_face),
        in_specs=[VMEM],
        out_specs=(VMEM, VMEM),
        compiler_params=params(),
        cost_estimate=pl.CostEstimate(flops=500_000_000, bytes_accessed=1_000_000, transcendentals=0),
        name="y_faces",
    )(flow)
    x_outer = exchanged(x_outer, EAST, True)
    y_outer = exchanged(y_outer, NORTH, True)
    y_inner = exchanged(y_inner, NORTH, False)
    x_inner = exchanged(x_inner, EAST, False)
    parts = pl.pallas_call(
        inner_kernel,
        out_shape=(jax.ShapeDtypeStruct((planes, rows, width), f32),) * 7,
        in_specs=[VMEM, VMEM],
        out_specs=(VMEM,) * 7,
        scratch_shapes=[pltpu.VMEM((3, rows + 16, width), f32)],
        compiler_params=params(),
        cost_estimate=pl.CostEstimate(flops=2_500_000_000, bytes_accessed=5_000_000, transcendentals=0),
        name="inner",
    )(flow, thermal)
    partial = pl.pallas_call(
        field_kernel,
        out_shape=jax.ShapeDtypeStruct((rows, planes * rank), f32),
        in_specs=[VMEM] * 12,
        out_specs=VMEM,
        compiler_params=params(),
        name="field",
    )(*parts, basis, x_outer, y_outer, y_inner, x_inner)
    north = lax.axis_size(NORTH)
    far = lax.axis_size(FAR)
    piece = rows // north
    depth = planes * rank
    gathered = lax.all_to_all(partial.reshape(north, piece, depth), NORTH, 0, 0)
    own, to_far = pl.pallas_call(
        sum_kernel,
        out_shape=(
            jax.ShapeDtypeStruct((1, piece, depth), jnp.bfloat16),
            jax.ShapeDtypeStruct((far, piece, depth), jnp.bfloat16),
        ),
        in_specs=[VMEM],
        out_specs=(VMEM, VMEM),
        compiler_params=params(),
        name="total",
    )(gathered)
    right = lax.all_to_all(to_far, FAR, 0, 0)
    own = pl.pallas_call(
        copy_kernel,
        out_shape=jax.ShapeDtypeStruct(own.shape, own.dtype),
        in_specs=[VMEM],
        out_specs=VMEM,
        compiler_params=params(),
        cost_estimate=pl.CostEstimate(flops=10_000_000_000, bytes_accessed=4 * piece * depth, transcendentals=0),
        name="own",
    )(own)
    near = jnp.concatenate([own] + [shifted(own, "x", -step) for step in range(1, 4)])
    across = shifted(near, "y_lo", 1)
    left = pl.pallas_call(
        arrange_kernel,
        out_shape=jax.ShapeDtypeStruct((north, piece, depth), jnp.bfloat16),
        in_specs=[VMEM] * 2,
        out_specs=VMEM,
        compiler_params=params(),
        cost_estimate=pl.CostEstimate(flops=5_000_000_000, bytes_accessed=4 * piece * depth * north, transcendentals=0),
        name="arrange",
    )(near, across)
    other = shifted(right, "core", 1)
    scale = 1.0 / depth
    block = pl.pallas_call(
        lambda *refs: block_kernel(scale, *refs),
        out_shape=jax.ShapeDtypeStruct((north, far * piece, 128), f32),
        in_specs=[VMEM] * 3,
        out_specs=VMEM,
        scratch_shapes=[pltpu.VMEM((2, far, piece, depth), jnp.bfloat16)],
        compiler_params=params(),
        name="block",
    )(left, right, other)
    blocks = lax.all_to_all(block, NORTH, 0, 0)
    return pl.pallas_call(
        lambda *refs: place_kernel(piece, *refs),
        out_shape=jax.ShapeDtypeStruct((rows, far * 128), f32),
        in_specs=[VMEM],
        out_specs=VMEM,
        compiler_params=params(),
        name="place",
    )(blocks)


def solution(mesh):
    fine = Mesh(mesh.devices.reshape(2, 8, 2, 4, 2), ("y_hi", "z", "core", "x", "y_lo"))
    placed = (P(None, None, EAST, NORTH), P(None, EAST, NORTH), P(NORTH, None))
    return jax.shard_map(body, mesh=fine, in_specs=placed, out_specs=P(EAST, None), check_vma=False)
```

```python
import jax
import jax.numpy as jnp
from jax import lax
from jax.experimental import pallas as pl
from jax.experimental.pallas import tpu as pltpu
from jax.sharding import Mesh
from jax.sharding import PartitionSpec as P

VMEM = pl.BlockSpec(memory_space=pltpu.VMEM)
FAR = ("y_hi", "z")
EAST = ("y_hi", "z", "core")
NORTH = ("x", "y_lo")
ORDER = (0, 3, 6, 1, 4, 7, 2, 5, 8, 11, 14, 9, 12, 15, 10, 13)
LIMIT = 48 * 1024 * 1024


def params():
    return pltpu.CompilerParams(vmem_limit_bytes=LIMIT)


def exchanged(value, axes, outer):
    count = lax.axis_size(axes)
    flip = [k ^ 1 for k in range(count)]
    if outer:
        flip = [(k + 1 if k % 2 else k - 1) % count for k in range(count)]
    return lax.ppermute(value, axes, list(enumerate(flip)))


def shifted(value, axes, step):
    count = lax.axis_size(axes)
    return lax.ppermute(value, axes, [(k, (k + step) % count) for k in range(count)])


def x_faces_kernel(flow, x_inner, x_outer, top, bottom, sems):
    planes, rows = x_inner.shape[1], flow.shape[2]
    middle = slice(2, planes + 2)
    copies = [
        pltpu.make_async_copy(flow.at[:, middle, 0:8], top, sems.at[0]),
        pltpu.make_async_copy(flow.at[:, middle, rows - 8 : rows], bottom, sems.at[1]),
    ]
    for copy in copies:
        copy.start()
    for copy in copies:
        copy.wait()
    x_even = lax.axis_index("core") == 0
    for comp in range(3):
        for plane in range(planes):
            first, last = top[comp, plane, 0:2], bottom[comp, plane, 6:8]
            x_inner[comp, plane] = jnp.where(x_even, last, first)
            x_outer[comp, plane] = jnp.where(x_even, first, last)


def y_faces_kernel(flow, y_inner, y_outer):
    planes, rows, width = flow.shape[1] - 4, flow.shape[2], flow.shape[3]
    y_even = lax.axis_index("y_lo") == 0
    lane = lax.broadcasted_iota(jnp.int32, (rows, 128), 1)
    first = jnp.zeros((rows, 128), jnp.float32)
    last = jnp.zeros((rows, 128), jnp.float32)
    for comp in range(3):
        for plane in range(planes):
            at = 2 * (comp * planes + plane)
            here = (lane == at) | (lane == at + 1)
            low = flow[comp, plane + 2, :, 0:128]
            high = flow[comp, plane + 2, :, width - 128 : width]
            first = jnp.where(here, pltpu.roll(low, at, 1) if at else low, first)
            last = jnp.where(here, pltpu.roll(high, (at + 2) % 128, 1), last)
    y_inner[:rows] = jnp.where(y_even, last, first)
    y_outer[:rows] = jnp.where(y_even, first, last)


def difference(ahead_two, ahead_one, behind_one, behind_two):
    return (8.0 * (ahead_one - behind_one) - (ahead_two - behind_two)) * (1.0 / 12.0)


def inner_kernel(flow, thermal, *refs):
    outs, padded = refs[:7], refs[7]
    planes = thermal.shape[0] - 4
    rows, width = thermal.shape[1], thermal.shape[2]
    total = width + 128
    none = jnp.zeros((rows, 128), jnp.float32)
    padded[:, 0:8, :] = jnp.zeros((3, 8, width), jnp.float32)
    padded[:, 8 + rows :, :] = jnp.zeros((3, 8, width), jnp.float32)
    for plane in range(planes):
        grads = []
        for comp in range(3):
            here = flow[comp, plane + 2]
            along_z = difference(
                flow[comp, plane + 4], flow[comp, plane + 3], flow[comp, plane + 1], flow[comp, plane]
            )
            padded[comp, 8 : 8 + rows, :] = here
            along_x = difference(
                padded[comp, 10 : 10 + rows, :],
                padded[comp, 9 : 9 + rows, :],
                padded[comp, 7 : 7 + rows, :],
                padded[comp, 6 : 6 + rows, :],
            )
            wide = jnp.concatenate([here, none], axis=1)
            along_y = difference(
                pltpu.roll(wide, total - 2, 1)[:, :width],
                pltpu.roll(wide, total - 1, 1)[:, :width],
                pltpu.roll(wide, 1, 1)[:, :width],
                pltpu.roll(wide, 2, 1)[:, :width],
            )
            grads.append((along_z, along_x, along_y))
        outs[0][plane] = grads[0][0]
        outs[1][plane] = grads[1][1]
        outs[2][plane] = grads[2][2]
        outs[3][plane] = grads[0][1] + grads[1][0]
        outs[4][plane] = grads[0][2] + grads[2][0]
        outs[5][plane] = grads[1][2] + grads[2][1]
        outs[6][plane] = 0.1 * jnp.exp(0.7 * jnp.log(thermal[plane + 2]))


def field_kernel(*refs):
    parts, basis = refs[:7], refs[7]
    x_outer, y_outer, y_inner, x_inner, out = refs[8:]
    planes, rows, width = parts[0].shape
    rank = basis.shape[1]
    matrix = basis[...]
    x_even, y_even = lax.axis_index("core") == 0, lax.axis_index("y_lo") == 0
    lane = lax.broadcasted_iota(jnp.int32, (rows, 128), 1)
    even = lane % 2 == 0
    y_low = jnp.where(y_even, y_outer[:rows], y_inner[:rows])
    y_high = jnp.where(y_even, y_inner[:rows], y_outer[:rows])
    y_low = jnp.where(even, y_low - 8.0 * pltpu.roll(y_low, 127, 1), y_low) * (1.0 / 12.0)
    y_high = jnp.where(even, -y_high, 8.0 * pltpu.roll(y_high, 1, 1) - y_high) * (1.0 / 12.0)
    blank = jnp.zeros((6, width), jnp.float32)

    def with_x(value, comp, plane):
        inner, outer = x_inner[comp, plane], x_outer[comp, plane]
        low = jnp.where(x_even, outer, inner)
        high = jnp.where(x_even, inner, outer)
        head = jnp.concatenate([low[0:1] - 8.0 * low[1:2], low[1:2], blank], axis=0)
        tail = jnp.concatenate([blank, -high[0:1], 8.0 * high[0:1] - high[1:2]], axis=0)
        return jnp.concatenate(
            [value[:8] + head * (1.0 / 12.0), value[8 : rows - 8], value[rows - 8 :] + tail * (1.0 / 12.0)],
            axis=0,
        )

    def with_y(value, comp, plane):
        at = 2 * (comp * planes + plane)
        low = pltpu.roll(y_low, 128 - at, 1) if at else y_low
        high = pltpu.roll(y_high, 126 - at, 1)
        return jnp.concatenate(
            [
                value[:, :128] + jnp.where(lane < 2, low, 0.0),
                        value[:, width - 128 :] + jnp.where(lane >= 126, high, 0.0),
            ],
            axis=1,
        )

    for plane in range(planes):
        along = parts[0][plane]
        down = with_x(parts[1][plane], 1, plane)
        over = with_y(parts[2][plane], 2, plane)
        cross_x = with_x(parts[3][plane], 0, plane)
        cross_y = with_y(parts[4][plane], 0, plane)
        cross_xy = with_x(with_y(parts[5][plane], 1, plane), 2, plane)
        expansion = along + down + over
        rate = (
            2.0 * (along * along + down * down + over * over)
            + (cross_x * cross_x + cross_y * cross_y + cross_xy * cross_xy)
            - (2.0 / 3.0) * (expansion * expansion)
        )
        field = parts[6][plane] * rate
        out[:, plane * rank : (plane + 1) * rank] = jnp.dot(
            field.astype(jnp.bfloat16), matrix, preferred_element_type=jnp.float32
        )


def sum_kernel(parts, own, far):
    total = parts[0]
    for part in range(1, parts.shape[0]):
        total = total + parts[part]
    piece = total.astype(jnp.bfloat16)
    own[0] = piece
    for at in range(far.shape[0]):
        far[at] = piece


def copy_kernel(source, target):
    target[...] = source[...]


def arrange_kernel(*refs):
    pairs, left = refs[:4], refs[4]
    x, y_lo = lax.axis_index("x"), lax.axis_index("y_lo")
    for step, pair in enumerate(pairs):
        at = 2 * lax.rem(x + step, 4)
        left[at + y_lo] = pair[0]
        left[at + 1 - y_lo] = pair[1]


def block_kernel(scale, left, own, other, out, right):
    core = lax.axis_index("core")
    count, piece, depth = own.shape
    a = left[...].reshape(left.shape[0] * piece, depth)
    half = count // 2
    for slot, at in enumerate(ORDER):
        right[core, at] = own[slot]
        right[1 - core, at] = other[slot]
    sides = []
    for side in range(2):
        w = right[:, side * half : (side + 1) * half].reshape(count * piece, depth)
        sides.append(lax.dot_general(w, a, (((1,), (1,)), ((), ())), preferred_element_type=jnp.float32))
    block = jnp.concatenate(sides, axis=1) * scale
    for at in range(out.shape[0]):
        out[at] = block


def place_kernel(piece, blocks, out):
    count, total, _ = blocks.shape
    tiles = total // (2 * piece)
    side = out.shape[0]
    for tile in range(tiles):
        rows = [
            blocks[at, (core * tiles + tile) * piece : (core * tiles + tile + 1) * piece, :]
            for core in range(2)
            for at in range(count)
        ]
        turned = jnp.concatenate(rows, axis=0).T
        out[:, tile * 128 : (tile + 1) * 128] = turned[:side]
        out[:, (tiles + tile) * 128 : (tiles + tile + 1) * 128] = turned[side:]


def body(flow, thermal, basis):
    planes = thermal.shape[0] - 4
    rows, width = thermal.shape[1], thermal.shape[2]
    rank = basis.shape[1]
    f32 = jnp.float32
    x_face = jax.ShapeDtypeStruct((3, planes, 2, width), f32)
    y_face = jax.ShapeDtypeStruct((rows + 16, 128), f32)
    x_inner, x_outer = pl.pallas_call(
        x_faces_kernel,
        out_shape=(x_face, x_face),
        in_specs=[pl.BlockSpec(memory_space=pltpu.HBM)],
        out_specs=(VMEM, VMEM),
        scratch_shapes=[
            pltpu.VMEM((3, planes, 8, width), f32),
            pltpu.VMEM((3, planes, 8, width), f32),
            pltpu.SemaphoreType.DMA((2,)),
        ],
        compiler_params=params(),
        name="x_faces",
    )(pltpu.with_memory_space_constraint(flow, pltpu.HBM))
    y_inner, y_outer = pl.pallas_call(
        y_faces_kernel,
        out_shape=(y_face, y_face),
        in_specs=[VMEM],
        out_specs=(VMEM, VMEM),
        compiler_params=params(),
        cost_estimate=pl.CostEstimate(flops=500_000_000, bytes_accessed=1_000_000, transcendentals=0),
        name="y_faces",
    )(flow)
    x_outer = exchanged(x_outer, EAST, True)
    y_outer = exchanged(y_outer, NORTH, True)
    y_inner = exchanged(y_inner, NORTH, False)
    x_inner = exchanged(x_inner, EAST, False)
    parts = pl.pallas_call(
        inner_kernel,
        out_shape=(jax.ShapeDtypeStruct((planes, rows, width), f32),) * 7,
        in_specs=[VMEM, VMEM],
        out_specs=(VMEM,) * 7,
        scratch_shapes=[pltpu.VMEM((3, rows + 16, width), f32)],
        compiler_params=params(),
        cost_estimate=pl.CostEstimate(flops=2_500_000_000, bytes_accessed=5_000_000, transcendentals=0),
        name="inner",
    )(flow, thermal)
    partial = pl.pallas_call(
        field_kernel,
        out_shape=jax.ShapeDtypeStruct((rows, planes * rank), f32),
        in_specs=[VMEM] * 12,
        out_specs=VMEM,
        compiler_params=params(),
        name="field",
    )(*parts, basis, x_outer, y_outer, y_inner, x_inner)
    north = lax.axis_size(NORTH)
    far = lax.axis_size(FAR)
    piece = rows // north
    depth = planes * rank
    gathered = lax.all_to_all(partial.reshape(north, piece, depth), NORTH, 0, 0)
    own, to_far = pl.pallas_call(
        sum_kernel,
        out_shape=(
            jax.ShapeDtypeStruct((1, piece, depth), jnp.bfloat16),
            jax.ShapeDtypeStruct((far, piece, depth), jnp.bfloat16),
        ),
        in_specs=[VMEM],
        out_specs=(VMEM, VMEM),
        compiler_params=params(),
        name="total",
    )(gathered)
    right = lax.all_to_all(to_far, FAR, 0, 0, axis_index_groups=[list(ORDER)])
    beside = shifted(own, "y_lo", 1)
    own = pl.pallas_call(
        copy_kernel,
        out_shape=jax.ShapeDtypeStruct(own.shape, own.dtype),
        in_specs=[VMEM],
        out_specs=VMEM,
        compiler_params=params(),
        cost_estimate=pl.CostEstimate(flops=10_000_000_000, bytes_accessed=4 * piece * depth, transcendentals=0),
        name="own",
    )(own)
    pair = jnp.concatenate([own, beside])
    pairs = [pair] + [shifted(pair, "x", -step) for step in range(1, 4)]
    left = pl.pallas_call(
        arrange_kernel,
        out_shape=jax.ShapeDtypeStruct((north, piece, depth), jnp.bfloat16),
        in_specs=[VMEM] * 4,
        out_specs=VMEM,
        compiler_params=params(),
        cost_estimate=pl.CostEstimate(flops=5_000_000_000, bytes_accessed=4 * piece * depth * north, transcendentals=0),
        name="arrange",
    )(*pairs)
    other = shifted(right, "core", 1)
    scale = 1.0 / depth
    block = pl.pallas_call(
        lambda *refs: block_kernel(scale, *refs),
        out_shape=jax.ShapeDtypeStruct((north, far * piece, 128), f32),
        in_specs=[VMEM] * 3,
        out_specs=VMEM,
        scratch_shapes=[pltpu.VMEM((2, far, piece, depth), jnp.bfloat16)],
        compiler_params=params(),
        name="block",
    )(left, right, other)
    blocks = lax.all_to_all(block, NORTH, 0, 0)
    return pl.pallas_call(
        lambda *refs: place_kernel(piece, *refs),
        out_shape=jax.ShapeDtypeStruct((rows, far * 128), f32),
        in_specs=[VMEM],
        out_specs=VMEM,
        compiler_params=params(),
        name="place",
    )(blocks)


def solution(mesh):
    fine = Mesh(mesh.devices.reshape(2, 8, 2, 4, 2), ("y_hi", "z", "core", "x", "y_lo"))
    placed = (P(None, None, EAST, NORTH), P(None, EAST, NORTH), P(NORTH, None))
    return jax.shard_map(body, mesh=fine, in_specs=placed, out_specs=P(EAST, None), check_vma=False)
```

```python
import jax
import jax.numpy as jnp
from jax import lax
from jax.experimental import pallas as pl
from jax.experimental.pallas import tpu as pltpu
from jax.sharding import Mesh
from jax.sharding import PartitionSpec as P

VMEM = pl.BlockSpec(memory_space=pltpu.VMEM)
FAR = ("y_hi", "z")
EAST = ("y_hi", "z", "core")
NORTH = ("x", "y_lo")
ORDER = (8, 11, 14, 9, 12, 15, 10, 13, 0, 3, 6, 1, 4, 7, 2, 5)
LIMIT = 48 * 1024 * 1024


def params():
    return pltpu.CompilerParams(vmem_limit_bytes=LIMIT)


def exchanged(value, axes, outer):
    count = lax.axis_size(axes)
    flip = [k ^ 1 for k in range(count)]
    if outer:
        flip = [(k + 1 if k % 2 else k - 1) % count for k in range(count)]
    return lax.ppermute(value, axes, list(enumerate(flip)))


def shifted(value, axes, step):
    count = lax.axis_size(axes)
    return lax.ppermute(value, axes, [(k, (k + step) % count) for k in range(count)])


def x_faces_kernel(flow, x_inner, x_outer, top, bottom, sems):
    planes, rows = x_inner.shape[1], flow.shape[2]
    middle = slice(2, planes + 2)
    copies = [
        pltpu.make_async_copy(flow.at[:, middle, 0:8], top, sems.at[0]),
        pltpu.make_async_copy(flow.at[:, middle, rows - 8 : rows], bottom, sems.at[1]),
    ]
    for copy in copies:
        copy.start()
    for copy in copies:
        copy.wait()
    x_even = lax.axis_index("core") == 0
    for comp in range(3):
        for plane in range(planes):
            first, last = top[comp, plane, 0:2], bottom[comp, plane, 6:8]
            x_inner[comp, plane] = jnp.where(x_even, last, first)
            x_outer[comp, plane] = jnp.where(x_even, first, last)


def y_faces_kernel(flow, y_inner, y_outer):
    planes, rows, width = flow.shape[1] - 4, flow.shape[2], flow.shape[3]
    y_even = lax.axis_index("y_lo") == 0
    lane = lax.broadcasted_iota(jnp.int32, (rows, 128), 1)
    first = jnp.zeros((rows, 128), jnp.float32)
    last = jnp.zeros((rows, 128), jnp.float32)
    for comp in range(3):
        for plane in range(planes):
            at = 2 * (comp * planes + plane)
            here = (lane == at) | (lane == at + 1)
            low = flow[comp, plane + 2, :, 0:128]
            high = flow[comp, plane + 2, :, width - 128 : width]
            first = jnp.where(here, pltpu.roll(low, at, 1) if at else low, first)
            last = jnp.where(here, pltpu.roll(high, (at + 2) % 128, 1), last)
    y_inner[:rows] = jnp.where(y_even, last, first)
    y_outer[:rows] = jnp.where(y_even, first, last)


def difference(ahead_two, ahead_one, behind_one, behind_two):
    return (8.0 * (ahead_one - behind_one) - (ahead_two - behind_two)) * (1.0 / 12.0)


def inner_kernel(flow, thermal, *refs):
    outs, padded = refs[:7], refs[7]
    planes = thermal.shape[0] - 4
    rows, width = thermal.shape[1], thermal.shape[2]
    total = width + 128
    none = jnp.zeros((rows, 128), jnp.float32)
    padded[:, 0:8, :] = jnp.zeros((3, 8, width), jnp.float32)
    padded[:, 8 + rows :, :] = jnp.zeros((3, 8, width), jnp.float32)
    for plane in range(planes):
        grads = []
        for comp in range(3):
            here = flow[comp, plane + 2]
            along_z = difference(
                flow[comp, plane + 4], flow[comp, plane + 3], flow[comp, plane + 1], flow[comp, plane]
            )
            padded[comp, 8 : 8 + rows, :] = here
            along_x = difference(
                padded[comp, 10 : 10 + rows, :],
                padded[comp, 9 : 9 + rows, :],
                padded[comp, 7 : 7 + rows, :],
                padded[comp, 6 : 6 + rows, :],
            )
            wide = jnp.concatenate([here, none], axis=1)
            along_y = difference(
                pltpu.roll(wide, total - 2, 1)[:, :width],
                pltpu.roll(wide, total - 1, 1)[:, :width],
                pltpu.roll(wide, 1, 1)[:, :width],
                pltpu.roll(wide, 2, 1)[:, :width],
            )
            grads.append((along_z, along_x, along_y))
        outs[0][plane] = grads[0][0]
        outs[1][plane] = grads[1][1]
        outs[2][plane] = grads[2][2]
        outs[3][plane] = grads[0][1] + grads[1][0]
        outs[4][plane] = grads[0][2] + grads[2][0]
        outs[5][plane] = grads[1][2] + grads[2][1]
        outs[6][plane] = 0.1 * jnp.exp(0.7 * jnp.log(thermal[plane + 2]))


def field_kernel(*refs):
    parts, basis = refs[:7], refs[7]
    x_outer, y_outer, y_inner, x_inner, out = refs[8:]
    planes, rows, width = parts[0].shape
    rank = basis.shape[1]
    matrix = basis[...]
    x_even, y_even = lax.axis_index("core") == 0, lax.axis_index("y_lo") == 0
    lane = lax.broadcasted_iota(jnp.int32, (rows, 128), 1)
    even = lane % 2 == 0
    y_low = jnp.where(y_even, y_outer[:rows], y_inner[:rows])
    y_high = jnp.where(y_even, y_inner[:rows], y_outer[:rows])
    y_low = jnp.where(even, y_low - 8.0 * pltpu.roll(y_low, 127, 1), y_low) * (1.0 / 12.0)
    y_high = jnp.where(even, -y_high, 8.0 * pltpu.roll(y_high, 1, 1) - y_high) * (1.0 / 12.0)
    blank = jnp.zeros((6, width), jnp.float32)

    def with_x(value, comp, plane):
        inner, outer = x_inner[comp, plane], x_outer[comp, plane]
        low = jnp.where(x_even, outer, inner)
        high = jnp.where(x_even, inner, outer)
        head = jnp.concatenate([low[0:1] - 8.0 * low[1:2], low[1:2], blank], axis=0)
        tail = jnp.concatenate([blank, -high[0:1], 8.0 * high[0:1] - high[1:2]], axis=0)
        return jnp.concatenate(
            [value[:8] + head * (1.0 / 12.0), value[8 : rows - 8], value[rows - 8 :] + tail * (1.0 / 12.0)],
            axis=0,
        )

    def with_y(value, comp, plane):
        at = 2 * (comp * planes + plane)
        low = pltpu.roll(y_low, 128 - at, 1) if at else y_low
        high = pltpu.roll(y_high, 126 - at, 1)
        return jnp.concatenate(
            [
                value[:, :128] + jnp.where(lane < 2, low, 0.0),
                        value[:, width - 128 :] + jnp.where(lane >= 126, high, 0.0),
            ],
            axis=1,
        )

    for plane in range(planes):
        along = parts[0][plane]
        down = with_x(parts[1][plane], 1, plane)
        over = with_y(parts[2][plane], 2, plane)
        cross_x = with_x(parts[3][plane], 0, plane)
        cross_y = with_y(parts[4][plane], 0, plane)
        cross_xy = with_x(with_y(parts[5][plane], 1, plane), 2, plane)
        expansion = along + down + over
        rate = (
            2.0 * (along * along + down * down + over * over)
            + (cross_x * cross_x + cross_y * cross_y + cross_xy * cross_xy)
            - (2.0 / 3.0) * (expansion * expansion)
        )
        field = parts[6][plane] * rate
        out[:, plane * rank : (plane + 1) * rank] = jnp.dot(
            field.astype(jnp.bfloat16), matrix, preferred_element_type=jnp.float32
        )


def sum_kernel(parts, own, far):
    total = parts[0]
    for part in range(1, parts.shape[0]):
        total = total + parts[part]
    piece = total.astype(jnp.bfloat16)
    own[0] = piece
    for at in range(far.shape[0]):
        far[at] = piece


def copy_kernel(source, target):
    target[...] = source[...]


def arrange_kernel(*refs):
    pairs, left = refs[:4], refs[4]
    x, y_lo = lax.axis_index("x"), lax.axis_index("y_lo")
    for step, pair in enumerate(pairs):
        at = 2 * lax.rem(x + step, 4)
        left[at + y_lo] = pair[0]
        left[at + 1 - y_lo] = pair[1]


def block_kernel(scale, left, own, other, out, right):
    core = lax.axis_index("core")
    count, piece, depth = own.shape
    a = left[...].reshape(left.shape[0] * piece, depth)
    half = count // 2
    for slot, at in enumerate(ORDER):
        right[core, at] = own[slot]
        right[1 - core, at] = other[slot]
    sides = []
    for side in range(2):
        w = right[:, side * half : (side + 1) * half].reshape(count * piece, depth)
        sides.append(lax.dot_general(w, a, (((1,), (1,)), ((), ())), preferred_element_type=jnp.float32))
    block = jnp.concatenate(sides, axis=1) * scale
    for at in range(out.shape[0]):
        out[at] = block


def place_kernel(piece, blocks, out):
    count, total, _ = blocks.shape
    tiles = total // (2 * piece)
    side = out.shape[0]
    for tile in range(tiles):
        rows = [
            blocks[at, (core * tiles + tile) * piece : (core * tiles + tile + 1) * piece, :]
            for core in range(2)
            for at in range(count)
        ]
        turned = jnp.concatenate(rows, axis=0).T
        out[:, tile * 128 : (tile + 1) * 128] = turned[:side]
        out[:, (tiles + tile) * 128 : (tiles + tile + 1) * 128] = turned[side:]


def body(flow, thermal, basis):
    planes = thermal.shape[0] - 4
    rows, width = thermal.shape[1], thermal.shape[2]
    rank = basis.shape[1]
    f32 = jnp.float32
    x_face = jax.ShapeDtypeStruct((3, planes, 2, width), f32)
    y_face = jax.ShapeDtypeStruct((rows + 16, 128), f32)
    x_inner, x_outer = pl.pallas_call(
        x_faces_kernel,
        out_shape=(x_face, x_face),
        in_specs=[pl.BlockSpec(memory_space=pltpu.HBM)],
        out_specs=(VMEM, VMEM),
        scratch_shapes=[
            pltpu.VMEM((3, planes, 8, width), f32),
            pltpu.VMEM((3, planes, 8, width), f32),
            pltpu.SemaphoreType.DMA((2,)),
        ],
        compiler_params=params(),
        name="x_faces",
    )(pltpu.with_memory_space_constraint(flow, pltpu.HBM))
    y_inner, y_outer = pl.pallas_call(
        y_faces_kernel,
        out_shape=(y_face, y_face),
        in_specs=[VMEM],
        out_specs=(VMEM, VMEM),
        compiler_params=params(),
        cost_estimate=pl.CostEstimate(flops=500_000_000, bytes_accessed=1_000_000, transcendentals=0),
        name="y_faces",
    )(flow)
    x_outer = exchanged(x_outer, EAST, True)
    y_outer = exchanged(y_outer, NORTH, True)
    y_inner = exchanged(y_inner, NORTH, False)
    x_inner = exchanged(x_inner, EAST, False)
    parts = pl.pallas_call(
        inner_kernel,
        out_shape=(jax.ShapeDtypeStruct((planes, rows, width), f32),) * 7,
        in_specs=[VMEM, VMEM],
        out_specs=(VMEM,) * 7,
        scratch_shapes=[pltpu.VMEM((3, rows + 16, width), f32)],
        compiler_params=params(),
        cost_estimate=pl.CostEstimate(flops=2_500_000_000, bytes_accessed=5_000_000, transcendentals=0),
        name="inner",
    )(flow, thermal)
    partial = pl.pallas_call(
        field_kernel,
        out_shape=jax.ShapeDtypeStruct((rows, planes * rank), f32),
        in_specs=[VMEM] * 12,
        out_specs=VMEM,
        compiler_params=params(),
        name="field",
    )(*parts, basis, x_outer, y_outer, y_inner, x_inner)
    north = lax.axis_size(NORTH)
    far = lax.axis_size(FAR)
    piece = rows // north
    depth = planes * rank
    gathered = lax.all_to_all(partial.reshape(north, piece, depth), NORTH, 0, 0)
    own, to_far = pl.pallas_call(
        sum_kernel,
        out_shape=(
            jax.ShapeDtypeStruct((1, piece, depth), jnp.bfloat16),
            jax.ShapeDtypeStruct((far, piece, depth), jnp.bfloat16),
        ),
        in_specs=[VMEM],
        out_specs=(VMEM, VMEM),
        compiler_params=params(),
        name="total",
    )(gathered)
    right = lax.all_to_all(to_far, FAR, 0, 0, axis_index_groups=[list(ORDER)])
    beside = shifted(own, "y_lo", 1)
    own = pl.pallas_call(
        copy_kernel,
        out_shape=jax.ShapeDtypeStruct(own.shape, own.dtype),
        in_specs=[VMEM],
        out_specs=VMEM,
        compiler_params=params(),
        cost_estimate=pl.CostEstimate(flops=10_000_000_000, bytes_accessed=4 * piece * depth, transcendentals=0),
        name="own",
    )(own)
    pair = jnp.concatenate([own, beside])
    pairs = [pair] + [shifted(pair, "x", -step) for step in range(1, 4)]
    left = pl.pallas_call(
        arrange_kernel,
        out_shape=jax.ShapeDtypeStruct((north, piece, depth), jnp.bfloat16),
        in_specs=[VMEM] * 4,
        out_specs=VMEM,
        compiler_params=params(),
        cost_estimate=pl.CostEstimate(flops=5_000_000_000, bytes_accessed=4 * piece * depth * north, transcendentals=0),
        name="arrange",
    )(*pairs)
    other = shifted(right, "core", 1)
    scale = 1.0 / depth
    block = pl.pallas_call(
        lambda *refs: block_kernel(scale, *refs),
        out_shape=jax.ShapeDtypeStruct((north, far * piece, 128), f32),
        in_specs=[VMEM] * 3,
        out_specs=VMEM,
        scratch_shapes=[pltpu.VMEM((2, far, piece, depth), jnp.bfloat16)],
        compiler_params=params(),
        name="block",
    )(left, right, other)
    blocks = lax.all_to_all(block, NORTH, 0, 0)
    return pl.pallas_call(
        lambda *refs: place_kernel(piece, *refs),
        out_shape=jax.ShapeDtypeStruct((rows, far * 128), f32),
        in_specs=[VMEM],
        out_specs=VMEM,
        compiler_params=params(),
        name="place",
    )(blocks)


def solution(mesh):
    fine = Mesh(mesh.devices.reshape(2, 8, 2, 4, 2), ("y_hi", "z", "core", "x", "y_lo"))
    placed = (P(None, None, EAST, NORTH), P(None, EAST, NORTH), P(NORTH, None))
    return jax.shard_map(body, mesh=fine, in_specs=placed, out_specs=P(EAST, None), check_vma=False)
```

```python
import jax
import jax.numpy as jnp
from jax import lax
from jax.experimental import pallas as pl
from jax.experimental.pallas import tpu as pltpu
from jax.sharding import Mesh
from jax.sharding import PartitionSpec as P

VMEM = pl.BlockSpec(memory_space=pltpu.VMEM)
FAR = ("y_hi", "z")
EAST = ("y_hi", "z", "core")
NORTH = ("x", "y_lo")
RING = (0, 3, 6, 1, 4, 7, 2, 5)
ORDER = tuple(8 + at for at in RING) + RING
LIMIT = 48 * 1024 * 1024


def params():
    return pltpu.CompilerParams(vmem_limit_bytes=LIMIT)


def exchanged(value, axes, outer):
    count = lax.axis_size(axes)
    flip = [k ^ 1 for k in range(count)]
    if outer:
        flip = [(k + 1 if k % 2 else k - 1) % count for k in range(count)]
    return lax.ppermute(value, axes, list(enumerate(flip)))


def shifted(value, axes, step):
    count = lax.axis_size(axes)
    return lax.ppermute(value, axes, [(k, (k + step) % count) for k in range(count)])


def x_faces_kernel(flow, x_inner, x_outer, top, bottom, sems):
    planes, rows = x_inner.shape[1], flow.shape[2]
    middle = slice(2, planes + 2)
    copies = [
        pltpu.make_async_copy(flow.at[:, middle, 0:8], top, sems.at[0]),
        pltpu.make_async_copy(flow.at[:, middle, rows - 8 : rows], bottom, sems.at[1]),
    ]
    for copy in copies:
        copy.start()
    for copy in copies:
        copy.wait()
    x_even = lax.axis_index("core") == 0
    for comp in range(3):
        for plane in range(planes):
            first, last = top[comp, plane, 0:2], bottom[comp, plane, 6:8]
            x_inner[comp, plane] = jnp.where(x_even, last, first)
            x_outer[comp, plane] = jnp.where(x_even, first, last)


def y_faces_kernel(flow, y_inner, y_outer):
    planes, rows, width = flow.shape[1] - 4, flow.shape[2], flow.shape[3]
    y_even = lax.axis_index("y_lo") == 0
    lane = lax.broadcasted_iota(jnp.int32, (rows, 128), 1)
    first = jnp.zeros((rows, 128), jnp.float32)
    last = jnp.zeros((rows, 128), jnp.float32)
    for comp in range(3):
        for plane in range(planes):
            at = 2 * (comp * planes + plane)
            here = (lane == at) | (lane == at + 1)
            low = flow[comp, plane + 2, :, 0:128]
            high = flow[comp, plane + 2, :, width - 128 : width]
            first = jnp.where(here, pltpu.roll(low, at, 1) if at else low, first)
            last = jnp.where(here, pltpu.roll(high, (at + 2) % 128, 1), last)
    y_inner[:rows] = jnp.where(y_even, last, first)
    y_outer[:rows] = jnp.where(y_even, first, last)


def difference(ahead_two, ahead_one, behind_one, behind_two):
    return (8.0 * (ahead_one - behind_one) - (ahead_two - behind_two)) * (1.0 / 12.0)


def inner_kernel(flow, thermal, *refs):
    outs, padded = refs[:7], refs[7]
    planes = thermal.shape[0] - 4
    rows, width = thermal.shape[1], thermal.shape[2]
    total = width + 128
    none = jnp.zeros((rows, 128), jnp.float32)
    padded[:, 0:8, :] = jnp.zeros((3, 8, width), jnp.float32)
    padded[:, 8 + rows :, :] = jnp.zeros((3, 8, width), jnp.float32)
    for plane in range(planes):
        grads = []
        for comp in range(3):
            here = flow[comp, plane + 2]
            along_z = difference(
                flow[comp, plane + 4], flow[comp, plane + 3], flow[comp, plane + 1], flow[comp, plane]
            )
            padded[comp, 8 : 8 + rows, :] = here
            along_x = difference(
                padded[comp, 10 : 10 + rows, :],
                padded[comp, 9 : 9 + rows, :],
                padded[comp, 7 : 7 + rows, :],
                padded[comp, 6 : 6 + rows, :],
            )
            wide = jnp.concatenate([here, none], axis=1)
            along_y = difference(
                pltpu.roll(wide, total - 2, 1)[:, :width],
                pltpu.roll(wide, total - 1, 1)[:, :width],
                pltpu.roll(wide, 1, 1)[:, :width],
                pltpu.roll(wide, 2, 1)[:, :width],
            )
            grads.append((along_z, along_x, along_y))
        outs[0][plane] = grads[0][0]
        outs[1][plane] = grads[1][1]
        outs[2][plane] = grads[2][2]
        outs[3][plane] = grads[0][1] + grads[1][0]
        outs[4][plane] = grads[0][2] + grads[2][0]
        outs[5][plane] = grads[1][2] + grads[2][1]
        outs[6][plane] = 0.1 * jnp.exp(0.7 * jnp.log(thermal[plane + 2]))


def field_kernel(*refs):
    parts, basis = refs[:7], refs[7]
    x_outer, y_outer, y_inner, x_inner, out = refs[8:]
    planes, rows, width = parts[0].shape
    rank = basis.shape[1]
    matrix = basis[...]
    x_even, y_even = lax.axis_index("core") == 0, lax.axis_index("y_lo") == 0
    lane = lax.broadcasted_iota(jnp.int32, (rows, 128), 1)
    even = lane % 2 == 0
    y_low = jnp.where(y_even, y_outer[:rows], y_inner[:rows])
    y_high = jnp.where(y_even, y_inner[:rows], y_outer[:rows])
    y_low = jnp.where(even, y_low - 8.0 * pltpu.roll(y_low, 127, 1), y_low) * (1.0 / 12.0)
    y_high = jnp.where(even, -y_high, 8.0 * pltpu.roll(y_high, 1, 1) - y_high) * (1.0 / 12.0)
    blank = jnp.zeros((6, width), jnp.float32)

    def with_x(value, comp, plane):
        inner, outer = x_inner[comp, plane], x_outer[comp, plane]
        low = jnp.where(x_even, outer, inner)
        high = jnp.where(x_even, inner, outer)
        head = jnp.concatenate([low[0:1] - 8.0 * low[1:2], low[1:2], blank], axis=0)
        tail = jnp.concatenate([blank, -high[0:1], 8.0 * high[0:1] - high[1:2]], axis=0)
        return jnp.concatenate(
            [value[:8] + head * (1.0 / 12.0), value[8 : rows - 8], value[rows - 8 :] + tail * (1.0 / 12.0)],
            axis=0,
        )

    def with_y(value, comp, plane):
        at = 2 * (comp * planes + plane)
        low = pltpu.roll(y_low, 128 - at, 1) if at else y_low
        high = pltpu.roll(y_high, 126 - at, 1)
        return jnp.concatenate(
            [
                value[:, :128] + jnp.where(lane < 2, low, 0.0),
                        value[:, width - 128 :] + jnp.where(lane >= 126, high, 0.0),
            ],
            axis=1,
        )

    for plane in range(planes):
        along = parts[0][plane]
        down = with_x(parts[1][plane], 1, plane)
        over = with_y(parts[2][plane], 2, plane)
        cross_x = with_x(parts[3][plane], 0, plane)
        cross_y = with_y(parts[4][plane], 0, plane)
        cross_xy = with_x(with_y(parts[5][plane], 1, plane), 2, plane)
        expansion = along + down + over
        rate = (
            2.0 * (along * along + down * down + over * over)
            + (cross_x * cross_x + cross_y * cross_y + cross_xy * cross_xy)
            - (2.0 / 3.0) * (expansion * expansion)
        )
        field = parts[6][plane] * rate
        out[:, plane * rank : (plane + 1) * rank] = jnp.dot(
            field.astype(jnp.bfloat16), matrix, preferred_element_type=jnp.float32
        )


def sum_kernel(parts, own, far):
    total = parts[0]
    for part in range(1, parts.shape[0]):
        total = total + parts[part]
    piece = total.astype(jnp.bfloat16)
    own[0] = piece
    for at in range(far.shape[0]):
        far[at] = piece


def copy_kernel(source, target):
    target[...] = source[...]


def products(rows, left, scale):
    count, piece, depth = rows.shape
    a = left[...].reshape(left.shape[0] * piece, depth)
    half = count // 2
    sides = []
    for slots in (slice(half, count), slice(0, half)):
        w = rows[slots].reshape(half * piece, depth)
        sides.append(lax.dot_general(w, a, (((1,), (1,)), ((), ())), preferred_element_type=jnp.float32))
    return jnp.concatenate(sides, axis=1) * scale


def arrange_kernel(scale, *refs):
    pairs, own, left, share = refs[:4], refs[4], refs[5], refs[6]
    x, y_lo = lax.axis_index("x"), lax.axis_index("y_lo")
    for step, pair in enumerate(pairs):
        at = 2 * lax.rem(x + step, 4)
        left[at + y_lo] = pair[0]
        left[at + 1 - y_lo] = pair[1]
    share[...] = products(own, left, scale)


def block_kernel(scale, left, share, other, out):
    core = lax.axis_index("core")
    mine, theirs = share[...], products(other, left, scale)
    size = mine.shape[0]
    near, away = pl.multiple_of(core * size, size), pl.multiple_of((1 - core) * size, size)
    for at in range(out.shape[0]):
        out[at, pl.ds(near, size)] = mine
        out[at, pl.ds(away, size)] = theirs


def place_kernel(piece, blocks, out):
    count, total, _ = blocks.shape
    tiles = total // (2 * piece)
    side = out.shape[0]
    for slot, tile in enumerate(RING):
        rows = [
            blocks[at, (core * tiles + slot) * piece : (core * tiles + slot + 1) * piece, :]
            for core in range(2)
            for at in range(count)
        ]
        turned = jnp.concatenate(rows, axis=0).T
        out[:, tile * 128 : (tile + 1) * 128] = turned[:side]
        out[:, (tiles + tile) * 128 : (tiles + tile + 1) * 128] = turned[side:]


def body(flow, thermal, basis):
    planes = thermal.shape[0] - 4
    rows, width = thermal.shape[1], thermal.shape[2]
    rank = basis.shape[1]
    f32 = jnp.float32
    x_face = jax.ShapeDtypeStruct((3, planes, 2, width), f32)
    y_face = jax.ShapeDtypeStruct((rows + 16, 128), f32)
    x_inner, x_outer = pl.pallas_call(
        x_faces_kernel,
        out_shape=(x_face, x_face),
        in_specs=[pl.BlockSpec(memory_space=pltpu.HBM)],
        out_specs=(VMEM, VMEM),
        scratch_shapes=[
            pltpu.VMEM((3, planes, 8, width), f32),
            pltpu.VMEM((3, planes, 8, width), f32),
            pltpu.SemaphoreType.DMA((2,)),
        ],
        compiler_params=params(),
        name="x_faces",
    )(pltpu.with_memory_space_constraint(flow, pltpu.HBM))
    y_inner, y_outer = pl.pallas_call(
        y_faces_kernel,
        out_shape=(y_face, y_face),
        in_specs=[VMEM],
        out_specs=(VMEM, VMEM),
        compiler_params=params(),
        cost_estimate=pl.CostEstimate(flops=500_000_000, bytes_accessed=1_000_000, transcendentals=0),
        name="y_faces",
    )(flow)
    x_outer = exchanged(x_outer, EAST, True)
    y_outer = exchanged(y_outer, NORTH, True)
    y_inner = exchanged(y_inner, NORTH, False)
    x_inner = exchanged(x_inner, EAST, False)
    parts = pl.pallas_call(
        inner_kernel,
        out_shape=(jax.ShapeDtypeStruct((planes, rows, width), f32),) * 7,
        in_specs=[VMEM, VMEM],
        out_specs=(VMEM,) * 7,
        scratch_shapes=[pltpu.VMEM((3, rows + 16, width), f32)],
        compiler_params=params(),
        cost_estimate=pl.CostEstimate(flops=2_500_000_000, bytes_accessed=5_000_000, transcendentals=0),
        name="inner",
    )(flow, thermal)
    partial = pl.pallas_call(
        field_kernel,
        out_shape=jax.ShapeDtypeStruct((rows, planes * rank), f32),
        in_specs=[VMEM] * 12,
        out_specs=VMEM,
        compiler_params=params(),
        name="field",
    )(*parts, basis, x_outer, y_outer, y_inner, x_inner)
    north = lax.axis_size(NORTH)
    far = lax.axis_size(FAR)
    piece = rows // north
    depth = planes * rank
    gathered = lax.all_to_all(partial.reshape(north, piece, depth), NORTH, 0, 0)
    own, to_far = pl.pallas_call(
        sum_kernel,
        out_shape=(
            jax.ShapeDtypeStruct((1, piece, depth), jnp.bfloat16),
            jax.ShapeDtypeStruct((far, piece, depth), jnp.bfloat16),
        ),
        in_specs=[VMEM],
        out_specs=(VMEM, VMEM),
        compiler_params=params(),
        name="total",
    )(gathered)
    right = lax.all_to_all(to_far, FAR, 0, 0, axis_index_groups=[list(ORDER)])
    beside = shifted(own, "y_lo", 1)
    own = pl.pallas_call(
        copy_kernel,
        out_shape=jax.ShapeDtypeStruct(own.shape, own.dtype),
        in_specs=[VMEM],
        out_specs=VMEM,
        compiler_params=params(),
        cost_estimate=pl.CostEstimate(flops=10_000_000_000, bytes_accessed=4 * piece * depth, transcendentals=0),
        name="own",
    )(own)
    pair = jnp.concatenate([own, beside])
    pairs = [pair] + [shifted(pair, "x", -step) for step in range(1, 4)]
    scale = 1.0 / depth
    left, share = pl.pallas_call(
        lambda *refs: arrange_kernel(scale, *refs),
        out_shape=(
            jax.ShapeDtypeStruct((north, piece, depth), jnp.bfloat16),
            jax.ShapeDtypeStruct((far * piece // 2, 128), f32),
        ),
        in_specs=[VMEM] * 5,
        out_specs=(VMEM, VMEM),
        compiler_params=params(),
        cost_estimate=pl.CostEstimate(flops=5_000_000_000, bytes_accessed=4 * piece * depth * north, transcendentals=0),
        name="arrange",
    )(*pairs, right)
    other = shifted(right, "core", 1)
    block = pl.pallas_call(
        lambda *refs: block_kernel(scale, *refs),
        out_shape=jax.ShapeDtypeStruct((north, far * piece, 128), f32),
        in_specs=[VMEM] * 3,
        out_specs=VMEM,
        compiler_params=params(),
        name="block",
    )(left, share, other)
    blocks = lax.all_to_all(block, NORTH, 0, 0)
    return pl.pallas_call(
        lambda *refs: place_kernel(piece, *refs),
        out_shape=jax.ShapeDtypeStruct((rows, far * 128), f32),
        in_specs=[VMEM],
        out_specs=VMEM,
        compiler_params=params(),
        name="place",
    )(blocks)


def solution(mesh):
    fine = Mesh(mesh.devices.reshape(2, 8, 2, 4, 2), ("y_hi", "z", "core", "x", "y_lo"))
    placed = (P(None, None, EAST, NORTH), P(None, EAST, NORTH), P(NORTH, None))
    return jax.shard_map(body, mesh=fine, in_specs=placed, out_specs=P(EAST, None), check_vma=False)
```

```python
import jax
import jax.numpy as jnp
from jax import lax
from jax.experimental import pallas as pl
from jax.experimental.pallas import tpu as pltpu
from jax.sharding import Mesh
from jax.sharding import PartitionSpec as P

VMEM = pl.BlockSpec(memory_space=pltpu.VMEM)
ANY = pl.BlockSpec(memory_space=pl.ANY)
FAR = ("y_hi", "z")
EAST = ("y_hi", "z", "core")
NORTH = ("x", "y_lo")
RING = (0, 3, 6, 1, 4, 7, 2, 5)
ORDER = tuple(8 + at for at in RING) + RING
LIMIT = 48 * 1024 * 1024


def params():
    return pltpu.CompilerParams(vmem_limit_bytes=LIMIT)


def exchanged(value, axes, outer):
    count = lax.axis_size(axes)
    flip = [k ^ 1 for k in range(count)]
    if outer:
        flip = [(k + 1 if k % 2 else k - 1) % count for k in range(count)]
    return lax.ppermute(value, axes, list(enumerate(flip)))


def shifted(value, axes, step):
    count = lax.axis_size(axes)
    return lax.ppermute(value, axes, [(k, (k + step) % count) for k in range(count)])


def x_faces_kernel(flow, x_outer, rows_held, sem):
    planes, rows = x_outer.shape[1], flow.shape[2]
    x_even = lax.axis_index("core") == 0
    start = pl.multiple_of(jnp.where(x_even, 0, rows - 8), 8)
    copy = pltpu.make_async_copy(
        flow.at[:, pl.ds(2, planes), pl.ds(start, 8)], rows_held, sem
    )
    copy.start()
    copy.wait()
    for comp in range(3):
        for plane in range(planes):
            held = rows_held[comp, plane]
            x_outer[comp, plane] = jnp.where(x_even, held[0:2], held[6:8])


def other_faces_kernel(flow, x_inner, y_inner, y_outer):
    planes, rows, width = flow.shape[1] - 4, flow.shape[2], flow.shape[3]
    x_even, y_even = lax.axis_index("core") == 0, lax.axis_index("y_lo") == 0
    lane = lax.broadcasted_iota(jnp.int32, (rows, 128), 1)
    first = jnp.zeros((rows, 128), jnp.float32)
    last = jnp.zeros((rows, 128), jnp.float32)
    for comp in range(3):
        for plane in range(planes):
            top = flow[comp, plane + 2, 0:2]
            bottom = flow[comp, plane + 2, rows - 2 : rows]
            x_inner[comp, plane, 0:2] = jnp.where(x_even, bottom, top)
            at = 2 * (comp * planes + plane)
            here = (lane == at) | (lane == at + 1)
            low = flow[comp, plane + 2, :, 0:128]
            high = flow[comp, plane + 2, :, width - 128 : width]
            first = jnp.where(here, pltpu.roll(low, at, 1) if at else low, first)
            last = jnp.where(here, pltpu.roll(high, (at + 2) % 128, 1), last)
    y_inner[:rows] = jnp.where(y_even, last, first)
    y_outer[:rows] = jnp.where(y_even, first, last)


def difference(ahead_two, ahead_one, behind_one, behind_two):
    return (8.0 * (ahead_one - behind_one) - (ahead_two - behind_two)) * (1.0 / 12.0)


def inner_kernel(flow, thermal, *refs):
    outs, padded = refs[:7], refs[7]
    planes = thermal.shape[0] - 4
    rows, width = thermal.shape[1], thermal.shape[2]
    total = width + 128
    none = jnp.zeros((rows, 128), jnp.float32)
    padded[:, 0:8, :] = jnp.zeros((3, 8, width), jnp.float32)
    padded[:, 8 + rows :, :] = jnp.zeros((3, 8, width), jnp.float32)
    for plane in range(planes):
        grads = []
        for comp in range(3):
            here = flow[comp, plane + 2]
            along_z = difference(
                flow[comp, plane + 4], flow[comp, plane + 3], flow[comp, plane + 1], flow[comp, plane]
            )
            padded[comp, 8 : 8 + rows, :] = here
            along_x = difference(
                padded[comp, 10 : 10 + rows, :],
                padded[comp, 9 : 9 + rows, :],
                padded[comp, 7 : 7 + rows, :],
                padded[comp, 6 : 6 + rows, :],
            )
            wide = jnp.concatenate([here, none], axis=1)
            along_y = difference(
                pltpu.roll(wide, total - 2, 1)[:, :width],
                pltpu.roll(wide, total - 1, 1)[:, :width],
                pltpu.roll(wide, 1, 1)[:, :width],
                pltpu.roll(wide, 2, 1)[:, :width],
            )
            grads.append((along_z, along_x, along_y))
        outs[0][plane] = grads[0][0]
        outs[1][plane] = grads[1][1]
        outs[2][plane] = grads[2][2]
        outs[3][plane] = grads[0][1] + grads[1][0]
        outs[4][plane] = grads[0][2] + grads[2][0]
        outs[5][plane] = grads[1][2] + grads[2][1]
        outs[6][plane] = 0.1 * jnp.exp(0.7 * jnp.log(thermal[plane + 2]))


def field_kernel(*refs):
    parts, basis = refs[:7], refs[7]
    x_outer, y_outer, y_inner, x_inner, out = refs[8:]
    planes, rows, width = parts[0].shape
    rank = basis.shape[1]
    matrix = basis[...]
    x_even, y_even = lax.axis_index("core") == 0, lax.axis_index("y_lo") == 0
    lane = lax.broadcasted_iota(jnp.int32, (rows, 128), 1)
    even = lane % 2 == 0
    y_low = jnp.where(y_even, y_outer[:rows], y_inner[:rows])
    y_high = jnp.where(y_even, y_inner[:rows], y_outer[:rows])
    y_low = jnp.where(even, y_low - 8.0 * pltpu.roll(y_low, 127, 1), y_low) * (1.0 / 12.0)
    y_high = jnp.where(even, -y_high, 8.0 * pltpu.roll(y_high, 1, 1) - y_high) * (1.0 / 12.0)
    blank = jnp.zeros((6, width), jnp.float32)

    def with_x(value, comp, plane):
        inner, outer = x_inner[comp, plane, 0:2], x_outer[comp, plane]
        low = jnp.where(x_even, outer, inner)
        high = jnp.where(x_even, inner, outer)
        head = jnp.concatenate([low[0:1] - 8.0 * low[1:2], low[1:2], blank], axis=0)
        tail = jnp.concatenate([blank, -high[0:1], 8.0 * high[0:1] - high[1:2]], axis=0)
        return jnp.concatenate(
            [value[:8] + head * (1.0 / 12.0), value[8 : rows - 8], value[rows - 8 :] + tail * (1.0 / 12.0)],
            axis=0,
        )

    def with_y(value, comp, plane):
        at = 2 * (comp * planes + plane)
        low = pltpu.roll(y_low, 128 - at, 1) if at else y_low
        high = pltpu.roll(y_high, 126 - at, 1)
        return jnp.concatenate(
            [
                value[:, :128] + jnp.where(lane < 2, low, 0.0),
                        value[:, width - 128 :] + jnp.where(lane >= 126, high, 0.0),
            ],
            axis=1,
        )

    for plane in range(planes):
        along = parts[0][plane]
        down = with_x(parts[1][plane], 1, plane)
        over = with_y(parts[2][plane], 2, plane)
        cross_x = with_x(parts[3][plane], 0, plane)
        cross_y = with_y(parts[4][plane], 0, plane)
        cross_xy = with_x(with_y(parts[5][plane], 1, plane), 2, plane)
        expansion = along + down + over
        rate = (
            2.0 * (along * along + down * down + over * over)
            + (cross_x * cross_x + cross_y * cross_y + cross_xy * cross_xy)
            - (2.0 / 3.0) * (expansion * expansion)
        )
        field = parts[6][plane] * rate
        out[:, plane * rank : (plane + 1) * rank] = jnp.dot(
            field.astype(jnp.bfloat16), matrix, preferred_element_type=jnp.float32
        )


def sum_kernel(parts, own, far):
    total = parts[0]
    for part in range(1, parts.shape[0]):
        total = total + parts[part]
    piece = total.astype(jnp.bfloat16)
    own[0] = piece
    for at in range(far.shape[0]):
        far[at] = piece


def copy_kernel(source, target):
    target[...] = source[...]


def products(rows, left, scale):
    count, piece, depth = rows.shape
    a = left[...].reshape(left.shape[0] * piece, depth)
    half = count // 2
    sides = []
    for slots in (slice(half, count), slice(0, half)):
        w = rows[slots].reshape(half * piece, depth)
        sides.append(lax.dot_general(w, a, (((1,), (1,)), ((), ())), preferred_element_type=jnp.float32))
    return jnp.concatenate(sides, axis=1) * scale


def arrange_kernel(scale, *refs):
    pairs, own, left, share = refs[:4], refs[4], refs[5], refs[6]
    x, y_lo = lax.axis_index("x"), lax.axis_index("y_lo")
    for step, pair in enumerate(pairs):
        at = 2 * lax.rem(x + step, 4)
        left[at + y_lo] = pair[0]
        left[at + 1 - y_lo] = pair[1]
    share[...] = products(own, left, scale)


def block_kernel(scale, left, share, other, out):
    core = lax.axis_index("core")
    mine, theirs = share[...], products(other, left, scale)
    size = mine.shape[0]
    near, away = pl.multiple_of(core * size, size), pl.multiple_of((1 - core) * size, size)
    for at in range(out.shape[0]):
        out[at, pl.ds(near, size)] = mine
        out[at, pl.ds(away, size)] = theirs


def place_kernel(piece, blocks, out):
    count, total, _ = blocks.shape
    tiles = total // (2 * piece)
    side = out.shape[0]
    for slot, tile in enumerate(RING):
        rows = [
            blocks[at, (core * tiles + slot) * piece : (core * tiles + slot + 1) * piece, :]
            for core in range(2)
            for at in range(count)
        ]
        turned = jnp.concatenate(rows, axis=0).T
        out[:, tile * 128 : (tile + 1) * 128] = turned[:side]
        out[:, (tiles + tile) * 128 : (tiles + tile + 1) * 128] = turned[side:]


def body(flow, thermal, basis):
    planes = thermal.shape[0] - 4
    rows, width = thermal.shape[1], thermal.shape[2]
    rank = basis.shape[1]
    f32 = jnp.float32
    x_face = jax.ShapeDtypeStruct((3, planes, 2, width), f32)
    y_face = jax.ShapeDtypeStruct((rows + 16, 128), f32)
    x_long = jax.ShapeDtypeStruct((3, planes, 2, width), f32)
    x_outer = pl.pallas_call(
        x_faces_kernel,
        out_shape=x_face,
        in_specs=[ANY],
        out_specs=VMEM,
        scratch_shapes=[pltpu.VMEM((3, planes, 8, width), f32), pltpu.SemaphoreType.DMA],
        compiler_params=params(),
        name="x_faces",
    )(pltpu.with_memory_space_constraint(flow, pltpu.HBM))
    x_inner, y_inner, y_outer = pl.pallas_call(
        other_faces_kernel,
        out_shape=(x_long, y_face, y_face),
        in_specs=[VMEM],
        out_specs=(VMEM,) * 3,
        compiler_params=params(),
        cost_estimate=pl.CostEstimate(flops=500_000_000, bytes_accessed=1_000_000, transcendentals=0),
        name="other_faces",
    )(flow)
    x_outer = exchanged(x_outer, EAST, True)
    y_outer = exchanged(y_outer, NORTH, True)
    y_inner = exchanged(y_inner, NORTH, False)
    x_inner = exchanged(x_inner, EAST, False)
    parts = pl.pallas_call(
        inner_kernel,
        out_shape=(jax.ShapeDtypeStruct((planes, rows, width), f32),) * 7,
        in_specs=[VMEM, VMEM],
        out_specs=(VMEM,) * 7,
        scratch_shapes=[pltpu.VMEM((3, rows + 16, width), f32)],
        compiler_params=params(),
        cost_estimate=pl.CostEstimate(flops=2_500_000_000, bytes_accessed=5_000_000, transcendentals=0),
        name="inner",
    )(flow, thermal)
    partial = pl.pallas_call(
        field_kernel,
        out_shape=jax.ShapeDtypeStruct((rows, planes * rank), f32),
        in_specs=[VMEM] * 12,
        out_specs=VMEM,
        compiler_params=params(),
        name="field",
    )(*parts, basis, x_outer, y_outer, y_inner, x_inner)
    north = lax.axis_size(NORTH)
    far = lax.axis_size(FAR)
    piece = rows // north
    depth = planes * rank
    gathered = lax.all_to_all(partial.reshape(north, piece, depth), NORTH, 0, 0)
    own, to_far = pl.pallas_call(
        sum_kernel,
        out_shape=(
            jax.ShapeDtypeStruct((1, piece, depth), jnp.bfloat16),
            jax.ShapeDtypeStruct((far, piece, depth), jnp.bfloat16),
        ),
        in_specs=[VMEM],
        out_specs=(VMEM, VMEM),
        compiler_params=params(),
        name="total",
    )(gathered)
    right = lax.all_to_all(to_far, FAR, 0, 0, axis_index_groups=[list(ORDER)])
    beside = shifted(own, "y_lo", 1)
    own = pl.pallas_call(
        copy_kernel,
        out_shape=jax.ShapeDtypeStruct(own.shape, own.dtype),
        in_specs=[VMEM],
        out_specs=VMEM,
        compiler_params=params(),
        cost_estimate=pl.CostEstimate(flops=10_000_000_000, bytes_accessed=4 * piece * depth, transcendentals=0),
        name="own",
    )(own)
    pair = jnp.concatenate([own, beside])
    pairs = [pair] + [shifted(pair, "x", -step) for step in range(1, 4)]
    scale = 1.0 / depth
    left, share = pl.pallas_call(
        lambda *refs: arrange_kernel(scale, *refs),
        out_shape=(
            jax.ShapeDtypeStruct((north, piece, depth), jnp.bfloat16),
            jax.ShapeDtypeStruct((far * piece // 2, 128), f32),
        ),
        in_specs=[VMEM] * 5,
        out_specs=(VMEM, VMEM),
        compiler_params=params(),
        cost_estimate=pl.CostEstimate(flops=5_000_000_000, bytes_accessed=4 * piece * depth * north, transcendentals=0),
        name="arrange",
    )(*pairs, right)
    other = shifted(right, "core", 1)
    block = pl.pallas_call(
        lambda *refs: block_kernel(scale, *refs),
        out_shape=jax.ShapeDtypeStruct((north, far * piece, 128), f32),
        in_specs=[VMEM] * 3,
        out_specs=VMEM,
        compiler_params=params(),
        name="block",
    )(left, share, other)
    blocks = lax.all_to_all(block, NORTH, 0, 0)
    return pl.pallas_call(
        lambda *refs: place_kernel(piece, *refs),
        out_shape=jax.ShapeDtypeStruct((rows, far * 128), f32),
        in_specs=[VMEM],
        out_specs=VMEM,
        compiler_params=params(),
        name="place",
    )(blocks)


def solution(mesh):
    fine = Mesh(mesh.devices.reshape(2, 8, 2, 4, 2), ("y_hi", "z", "core", "x", "y_lo"))
    placed = (P(None, None, EAST, NORTH), P(None, EAST, NORTH), P(NORTH, None))
    return jax.shard_map(body, mesh=fine, in_specs=placed, out_specs=P(EAST, None), check_vma=False)
```

```python
import jax
import jax.numpy as jnp
from jax import lax
from jax.experimental import pallas as pl
from jax.experimental.pallas import tpu as pltpu
from jax.sharding import Mesh
from jax.sharding import PartitionSpec as P

VMEM = pl.BlockSpec(memory_space=pltpu.VMEM)
ANY = pl.BlockSpec(memory_space=pl.ANY)
FAR = ("y_hi", "z")
EAST = ("y_hi", "z", "core")
NORTH = ("x", "y_lo")
RING = (0, 3, 6, 1, 4, 7, 2, 5)
ORDER = tuple(8 + at for at in RING) + RING
LIMIT = 48 * 1024 * 1024


def params():
    return pltpu.CompilerParams(vmem_limit_bytes=LIMIT)


def exchanged(value, axes, outer):
    count = lax.axis_size(axes)
    flip = [k ^ 1 for k in range(count)]
    if outer:
        flip = [(k + 1 if k % 2 else k - 1) % count for k in range(count)]
    return lax.ppermute(value, axes, list(enumerate(flip)))


def shifted(value, axes, step):
    count = lax.axis_size(axes)
    return lax.ppermute(value, axes, [(k, (k + step) % count) for k in range(count)])


def x_faces_kernel(flow, x_outer, rows_held, sem):
    planes, rows = x_outer.shape[1], flow.shape[2]
    x_even = lax.axis_index("core") == 0
    start = pl.multiple_of(jnp.where(x_even, 0, rows - 8), 8)
    copy = pltpu.make_async_copy(
        flow.at[:, pl.ds(2, planes), pl.ds(start, 8)], rows_held, sem
    )
    copy.start()
    copy.wait()
    for comp in range(3):
        for plane in range(planes):
            held = rows_held[comp, plane]
            x_outer[comp, plane] = jnp.where(x_even, held[0:2], held[6:8])


def other_faces_kernel(flow, x_inner, y_inner, y_outer):
    planes, rows, width = flow.shape[1] - 4, flow.shape[2], flow.shape[3]
    x_even, y_even = lax.axis_index("core") == 0, lax.axis_index("y_lo") == 0
    lane = lax.broadcasted_iota(jnp.int32, (rows, 128), 1)
    first = jnp.zeros((rows, 128), jnp.float32)
    last = jnp.zeros((rows, 128), jnp.float32)
    for comp in range(3):
        for plane in range(planes):
            top = flow[comp, plane + 2, 0:2]
            bottom = flow[comp, plane + 2, rows - 2 : rows]
            x_inner[comp, plane, 0:2] = jnp.where(x_even, bottom, top)
            at = 2 * (comp * planes + plane)
            here = (lane == at) | (lane == at + 1)
            low = flow[comp, plane + 2, :, 0:128]
            high = flow[comp, plane + 2, :, width - 128 : width]
            first = jnp.where(here, pltpu.roll(low, at, 1) if at else low, first)
            last = jnp.where(here, pltpu.roll(high, (at + 2) % 128, 1), last)
    y_inner[:rows] = jnp.where(y_even, last, first)
    y_outer[:rows] = jnp.where(y_even, first, last)


def difference(ahead_two, ahead_one, behind_one, behind_two):
    return (8.0 * (ahead_one - behind_one) - (ahead_two - behind_two)) * (1.0 / 12.0)


def inner_kernel(flow, thermal, *refs):
    outs, padded = refs[:7], refs[7]
    planes = thermal.shape[0] - 4
    rows, width = thermal.shape[1], thermal.shape[2]
    total = width + 128
    none = jnp.zeros((rows, 128), jnp.float32)
    padded[:, 0:8, :] = jnp.zeros((3, 8, width), jnp.float32)
    padded[:, 8 + rows :, :] = jnp.zeros((3, 8, width), jnp.float32)
    for plane in range(planes):
        grads = []
        for comp in range(3):
            here = flow[comp, plane + 2]
            along_z = difference(
                flow[comp, plane + 4], flow[comp, plane + 3], flow[comp, plane + 1], flow[comp, plane]
            )
            padded[comp, 8 : 8 + rows, :] = here
            along_x = difference(
                padded[comp, 10 : 10 + rows, :],
                padded[comp, 9 : 9 + rows, :],
                padded[comp, 7 : 7 + rows, :],
                padded[comp, 6 : 6 + rows, :],
            )
            wide = jnp.concatenate([here, none], axis=1)
            along_y = difference(
                pltpu.roll(wide, total - 2, 1)[:, :width],
                pltpu.roll(wide, total - 1, 1)[:, :width],
                pltpu.roll(wide, 1, 1)[:, :width],
                pltpu.roll(wide, 2, 1)[:, :width],
            )
            grads.append((along_z, along_x, along_y))
        outs[0][plane] = grads[0][0]
        outs[1][plane] = grads[1][1]
        outs[2][plane] = grads[2][2]
        outs[3][plane] = grads[0][1] + grads[1][0]
        outs[4][plane] = grads[0][2] + grads[2][0]
        outs[5][plane] = grads[1][2] + grads[2][1]
        outs[6][plane] = 0.1 * jnp.exp(0.7 * jnp.log(thermal[plane + 2]))


def field_kernel(*refs):
    parts, basis = refs[:7], refs[7]
    x_outer, y_outer, y_inner, x_inner, out = refs[8:]
    planes, rows, width = parts[0].shape
    rank = basis.shape[1]
    matrix = basis[...]
    x_even, y_even = lax.axis_index("core") == 0, lax.axis_index("y_lo") == 0
    lane = lax.broadcasted_iota(jnp.int32, (rows, 128), 1)
    even = lane % 2 == 0
    y_low = jnp.where(y_even, y_outer[:rows], y_inner[:rows])
    y_high = jnp.where(y_even, y_inner[:rows], y_outer[:rows])
    y_low = jnp.where(even, y_low - 8.0 * pltpu.roll(y_low, 127, 1), y_low) * (1.0 / 12.0)
    y_high = jnp.where(even, -y_high, 8.0 * pltpu.roll(y_high, 1, 1) - y_high) * (1.0 / 12.0)
    blank = jnp.zeros((6, width), jnp.float32)

    def with_x(value, comp, plane):
        inner, outer = x_inner[comp, plane, 0:2], x_outer[comp, plane]
        low = jnp.where(x_even, outer, inner)
        high = jnp.where(x_even, inner, outer)
        head = jnp.concatenate([low[0:1] - 8.0 * low[1:2], low[1:2], blank], axis=0)
        tail = jnp.concatenate([blank, -high[0:1], 8.0 * high[0:1] - high[1:2]], axis=0)
        return jnp.concatenate(
            [value[:8] + head * (1.0 / 12.0), value[8 : rows - 8], value[rows - 8 :] + tail * (1.0 / 12.0)],
            axis=0,
        )

    def with_y(value, comp, plane):
        at = 2 * (comp * planes + plane)
        low = pltpu.roll(y_low, 128 - at, 1) if at else y_low
        high = pltpu.roll(y_high, 126 - at, 1)
        return jnp.concatenate(
            [
                value[:, :128] + jnp.where(lane < 2, low, 0.0),
                        value[:, width - 128 :] + jnp.where(lane >= 126, high, 0.0),
            ],
            axis=1,
        )

    for plane in range(planes):
        along = parts[0][plane]
        down = with_x(parts[1][plane], 1, plane)
        over = with_y(parts[2][plane], 2, plane)
        cross_x = with_x(parts[3][plane], 0, plane)
        cross_y = with_y(parts[4][plane], 0, plane)
        cross_xy = with_x(with_y(parts[5][plane], 1, plane), 2, plane)
        expansion = along + down + over
        rate = (
            2.0 * (along * along + down * down + over * over)
            + (cross_x * cross_x + cross_y * cross_y + cross_xy * cross_xy)
            - (2.0 / 3.0) * (expansion * expansion)
        )
        field = parts[6][plane] * rate
        out[:, plane * rank : (plane + 1) * rank] = jnp.dot(
            field.astype(jnp.bfloat16), matrix, preferred_element_type=jnp.float32
        )


def sum_kernel(parts, own, far):
    total = parts[0]
    for part in range(1, parts.shape[0]):
        total = total + parts[part]
    piece = total.astype(jnp.bfloat16)
    own[0] = piece
    for at in range(far.shape[0]):
        far[at] = piece


def copy_kernel(source, target):
    target[...] = source[...]


def products(rows, left, scale):
    count, piece, depth = rows.shape
    a = left[...].reshape(left.shape[0] * piece, depth)
    half = count // 2
    sides = []
    for slots in (slice(half, count), slice(0, half)):
        w = rows[slots].reshape(half * piece, depth)
        sides.append(lax.dot_general(w, a, (((1,), (1,)), ((), ())), preferred_element_type=jnp.float32))
    return jnp.concatenate(sides, axis=1) * scale


def arrange_kernel(scale, *refs):
    pairs, own, left, share = refs[:4], refs[4], refs[5], refs[6]
    x, y_lo = lax.axis_index("x"), lax.axis_index("y_lo")
    for step, pair in zip((0, 1, 3, 2), pairs):
        at = 2 * lax.rem(x + step, 4)
        left[at + y_lo] = pair[0]
        left[at + 1 - y_lo] = pair[1]
    share[...] = products(own, left, scale)


def block_kernel(scale, left, share, other, out):
    core = lax.axis_index("core")
    mine, theirs = share[...], products(other, left, scale)
    size = mine.shape[0]
    near, away = pl.multiple_of(core * size, size), pl.multiple_of((1 - core) * size, size)
    for at in range(out.shape[0]):
        out[at, pl.ds(near, size)] = mine
        out[at, pl.ds(away, size)] = theirs


def place_kernel(piece, blocks, out):
    count, total, _ = blocks.shape
    tiles = total // (2 * piece)
    side = out.shape[0]
    for slot, tile in enumerate(RING):
        rows = [
            blocks[at, (core * tiles + slot) * piece : (core * tiles + slot + 1) * piece, :]
            for core in range(2)
            for at in range(count)
        ]
        turned = jnp.concatenate(rows, axis=0).T
        out[:, tile * 128 : (tile + 1) * 128] = turned[:side]
        out[:, (tiles + tile) * 128 : (tiles + tile + 1) * 128] = turned[side:]


def body(flow, thermal, basis):
    planes = thermal.shape[0] - 4
    rows, width = thermal.shape[1], thermal.shape[2]
    rank = basis.shape[1]
    f32 = jnp.float32
    x_face = jax.ShapeDtypeStruct((3, planes, 2, width), f32)
    y_face = jax.ShapeDtypeStruct((rows + 16, 128), f32)
    x_long = jax.ShapeDtypeStruct((3, planes, 2, width), f32)
    x_outer = pl.pallas_call(
        x_faces_kernel,
        out_shape=x_face,
        in_specs=[ANY],
        out_specs=VMEM,
        scratch_shapes=[pltpu.VMEM((3, planes, 8, width), f32), pltpu.SemaphoreType.DMA],
        compiler_params=params(),
        name="x_faces",
    )(pltpu.with_memory_space_constraint(flow, pltpu.HBM))
    x_inner, y_inner, y_outer = pl.pallas_call(
        other_faces_kernel,
        out_shape=(x_long, y_face, y_face),
        in_specs=[VMEM],
        out_specs=(VMEM,) * 3,
        compiler_params=params(),
        cost_estimate=pl.CostEstimate(flops=500_000_000, bytes_accessed=1_000_000, transcendentals=0),
        name="other_faces",
    )(flow)
    x_outer = exchanged(x_outer, EAST, True)
    y_outer = exchanged(y_outer, NORTH, True)
    y_inner = exchanged(y_inner, NORTH, False)
    x_inner = exchanged(x_inner, EAST, False)
    parts = pl.pallas_call(
        inner_kernel,
        out_shape=(jax.ShapeDtypeStruct((planes, rows, width), f32),) * 7,
        in_specs=[VMEM, VMEM],
        out_specs=(VMEM,) * 7,
        scratch_shapes=[pltpu.VMEM((3, rows + 16, width), f32)],
        compiler_params=params(),
        cost_estimate=pl.CostEstimate(flops=2_500_000_000, bytes_accessed=5_000_000, transcendentals=0),
        name="inner",
    )(flow, thermal)
    partial = pl.pallas_call(
        field_kernel,
        out_shape=jax.ShapeDtypeStruct((rows, planes * rank), f32),
        in_specs=[VMEM] * 12,
        out_specs=VMEM,
        compiler_params=params(),
        name="field",
    )(*parts, basis, x_outer, y_outer, y_inner, x_inner)
    north = lax.axis_size(NORTH)
    far = lax.axis_size(FAR)
    piece = rows // north
    depth = planes * rank
    gathered = lax.all_to_all(partial.reshape(north, piece, depth), NORTH, 0, 0)
    own, to_far = pl.pallas_call(
        sum_kernel,
        out_shape=(
            jax.ShapeDtypeStruct((1, piece, depth), jnp.bfloat16),
            jax.ShapeDtypeStruct((far, piece, depth), jnp.bfloat16),
        ),
        in_specs=[VMEM],
        out_specs=(VMEM, VMEM),
        compiler_params=params(),
        name="total",
    )(gathered)
    right = lax.all_to_all(to_far, FAR, 0, 0, axis_index_groups=[list(ORDER)])
    beside = shifted(own, "y_lo", 1)
    own = pl.pallas_call(
        copy_kernel,
        out_shape=jax.ShapeDtypeStruct(own.shape, own.dtype),
        in_specs=[VMEM],
        out_specs=VMEM,
        compiler_params=params(),
        cost_estimate=pl.CostEstimate(flops=10_000_000_000, bytes_accessed=4 * piece * depth, transcendentals=0),
        name="own",
    )(own)
    pair = jnp.concatenate([own, beside])
    pairs = [pair] + [shifted(pair, "x", -step) for step in (1, 3, 2)]
    scale = 1.0 / depth
    left, share = pl.pallas_call(
        lambda *refs: arrange_kernel(scale, *refs),
        out_shape=(
            jax.ShapeDtypeStruct((north, piece, depth), jnp.bfloat16),
            jax.ShapeDtypeStruct((far * piece // 2, 128), f32),
        ),
        in_specs=[VMEM] * 5,
        out_specs=(VMEM, VMEM),
        compiler_params=params(),
        cost_estimate=pl.CostEstimate(flops=5_000_000_000, bytes_accessed=4 * piece * depth * north, transcendentals=0),
        name="arrange",
    )(*pairs, right)
    other = shifted(right, "core", 1)
    block = pl.pallas_call(
        lambda *refs: block_kernel(scale, *refs),
        out_shape=jax.ShapeDtypeStruct((north, far * piece, 128), f32),
        in_specs=[VMEM] * 3,
        out_specs=VMEM,
        compiler_params=params(),
        name="block",
    )(left, share, other)
    blocks = lax.all_to_all(block, NORTH, 0, 0)
    return pl.pallas_call(
        lambda *refs: place_kernel(piece, *refs),
        out_shape=jax.ShapeDtypeStruct((rows, far * 128), f32),
        in_specs=[VMEM],
        out_specs=VMEM,
        compiler_params=params(),
        name="place",
    )(blocks)


def solution(mesh):
    fine = Mesh(mesh.devices.reshape(2, 8, 2, 4, 2), ("y_hi", "z", "core", "x", "y_lo"))
    placed = (P(None, None, EAST, NORTH), P(None, EAST, NORTH), P(NORTH, None))
    return jax.shard_map(body, mesh=fine, in_specs=placed, out_specs=P(EAST, None), check_vma=False)
```
